32 devices in a mesh: section: 4 (over z), dp: 8 (over y, x, core).
Axes of the slice: x: 2, y: 2, z: 4, core: 2. Of those that a mesh axis runs over, the one named last changes fastest.
Arguments:
- master: float32 [4, 2560, 2560], P('section', 'dp'), may hold values from -0.125 to 0.125
- first_moment: float32 [4, 2560, 2560], P('section', 'dp'), may hold values from -3 to 3
- second_moment: float32 [4, 2560, 2560], P('section', 'dp'), may hold values from 0.1 to 4
- inputs_own: bfloat16 [4, 4, 1024, 2560], P('section', None, 'dp'), may hold values from -6 to 6
- inputs_arriving: bfloat16 [4, 4, 1024, 2560], P('section', None, 'dp'), may hold values from -6 to 6
- grads_own: bfloat16 [4, 4, 1024, 2560], P('section', None, 'dp'), may hold values from -0.1875 to 0.1875
- windows_own: int32 [4, 1024, 2560], P('section', 'dp'), may hold values from 0 to 15
- windows_arriving: int32 [4, 1024, 2560], P('section', 'dp'), may hold values from 0 to 15
- next_inputs: bfloat16 [4, 256, 2560], P('section', 'dp'), may hold values from -6 to 6
Outputs:
- fresh_params: float32 [4, 2560, 2560], P('section', 'dp')
- fresh_first: float32 [4, 2560, 2560], P('section', 'dp')
- fresh_second: float32 [4, 2560, 2560], P('section', 'dp')
- next_currents: bfloat16 [4, 256, 2560], P('section', 'dp')
The draws below stay inside these ranges and needn't reach their ends.
Inputs may be any that keep to these rules, and one draw needn't show every extreme that they name: `windows_own`: bit t of an entry is the surrogate derivative of spikes_t by v_t for timestep t. `windows_arriving`: bit t of an entry is the surrogate derivative of spikes_t by v_t for timestep t.
All inputs are finite; a program needn't handle non-finite values.
Results may differ from the reference program's by a relative error of at most 0.008.
Values may be sent and summed in bfloat16 or wider, within the bound.
No kernel may reach another device: no remote copies, remote signals or barrier semaphores. Data moves between devices by JAX's collectives and lax.ppermute only.
A program may use at most 128 MiB of HBM per device.

```python
import math
import jax
import jax.numpy as jnp
from jax import lax

FEATURES = 2560
TIMESTEPS = 4
TOK_DEV = 128
SECTIONS = 4
TOKENS = 1024
NEXT_TOKENS = 256
N_DP = 8


def touch_ends(entries, key, low, high):
    longest = entries.shape.index(max(entries.shape))
    spots = []
    for shift in (0, 1):
        where = [jax.random.randint(jax.random.fold_in(key, axis), (), 0, length) for axis, length in enumerate(entries.shape)]
        where[longest] = (where[longest] + shift) % entries.shape[longest]
        spots.append(tuple(where))
    return entries.at[spots[0]].set(low).at[spots[1]].set(high)


def shard_levels(key, dims, split, smallest, high):
    def one(position, shards_of):
        steps = jax.random.uniform(jax.random.fold_in(jax.random.fold_in(key, 6), position), (shards_of,), jnp.float32, smallest / len(split), high / len(split))
        return jnp.repeat(jnp.exp(steps), dims[position] // shards_of).reshape((-1,) + (1,) * (len(dims) - position - 1))

    level = one(*split[0])
    for cut in split[1:]:
        level = level * one(*cut)
    return level


def bell_draw(key, extent, scale, most, shards=(), held_as=jnp.bfloat16):
    loudness = shard_levels(key, extent, shards, -0.22, 0.18) if shards else 1.0
    drawn = jax.random.normal(key, extent, jnp.float32) * scale * loudness
    return jnp.minimum(jnp.maximum(drawn, -most), most).astype(held_as)


def setup_inputs(seed: int = 0) -> dict:
    streams_of = jax.random.split(jax.random.key(seed), 10)
    return {
        "master": bell_draw(streams_of[0], (SECTIONS, FEATURES, FEATURES), FEATURES ** -0.5, 0.125, ((0, 4), (1, 8)), jnp.float32),
        "first_moment": bell_draw(streams_of[1], (SECTIONS, FEATURES, FEATURES), 0.5, 3.0, ((0, 4), (1, 8)), jnp.float32),
        "second_moment": jnp.clip(jnp.exp(math.log(4.0) - 3.6888794 * jax.random.uniform(streams_of[2], (SECTIONS, FEATURES, FEATURES), jnp.float32) ** shard_levels(streams_of[2], (SECTIONS, FEATURES, FEATURES), ((0, 4), (1, 8)), -0.2, 0.2)), 0.1, 4.0),
        "inputs_own": bell_draw(streams_of[3], (SECTIONS, TIMESTEPS, TOKENS, FEATURES), 1.0, 6.0, ((0, 4), (2, 8))),
        "inputs_arriving": bell_draw(streams_of[4], (SECTIONS, TIMESTEPS, TOKENS, FEATURES), 1.0, 6.0, ((0, 4), (2, 8))),
        "grads_own": bell_draw(streams_of[5], (SECTIONS, TIMESTEPS, TOKENS, FEATURES), (2 * (TIMESTEPS * TOKENS) ** -0.5), 0.1875, ((0, 4), (2, 8))),
        "windows_own": touch_ends(jax.random.randint(streams_of[6], (SECTIONS, TOKENS, FEATURES), 0, 2 ** TIMESTEPS), jax.random.fold_in(streams_of[6], 1), 0, (2 ** TIMESTEPS) - 1).astype(jnp.int32),
        "windows_arriving": touch_ends(jax.random.randint(streams_of[7], (SECTIONS, TOKENS, FEATURES), 0, 2 ** TIMESTEPS), jax.random.fold_in(streams_of[7], 1), 0, (2 ** TIMESTEPS) - 1).astype(jnp.int32),
        "next_inputs": bell_draw(streams_of[8], (SECTIONS, NEXT_TOKENS, FEATURES), 1.0, 6.0, ((0, 4), (1, 8))),
    }


LEAK_RATE = 0.5
LEARN_RATE = 0.002
FIRST_DECAY = 0.9
SECOND_DECAY = 0.95
EPSILON = 1e-08
WEIGHT_DECAY = 0.1
FIRST_CORRECTION = 1.0 - 0.9 ** 10
SECOND_CORRECTION = 1.0 - 0.95 ** 10

def membrane_grads(gradients, windows):
    carried = jnp.zeros(gradients.shape[1:], jnp.float32)
    results = []
    for moment in reversed(range(gradients.shape[0])):
        window = jnp.bitwise_and(jnp.right_shift(windows, moment), 1).astype(jnp.float32)
        carried = window * gradients[moment].astype(jnp.float32) + LEAK_RATE * carried
        results = [carried] + results
    return jnp.stack(results).astype(jnp.bfloat16)

def send_grad(bundle):
    params, gradients, windows = bundle
    membrane = membrane_grads(gradients, windows).reshape(TIMESTEPS * TOKENS, FEATURES)
    through = jnp.dot(membrane, params.astype(jnp.bfloat16).T, preferred_element_type=jnp.float32)
    summed = gradients.reshape(TIMESTEPS * TOKENS, FEATURES).astype(jnp.float32) + through
    return summed.astype(jnp.bfloat16).reshape(TIMESTEPS, TOKENS, FEATURES)

def update_section(bundle):
    params, first_old, second_old, acts_own, acts_arriving, grads_now, windows_now, received, windows_later, upcoming = bundle
    membrane_own = membrane_grads(grads_now, windows_now)
    membrane_arriving = membrane_grads(received, windows_later)

    def shard_term(shard_index, running):
        offset = (shard_index * TOK_DEV).astype(jnp.int32)

        def flatten_rows(values):
            return lax.dynamic_slice_in_dim(values, offset, TOK_DEV, 1).reshape(TIMESTEPS * TOK_DEV, FEATURES)
        partial_value = jnp.dot(flatten_rows(acts_own).T, flatten_rows(membrane_own), preferred_element_type=jnp.float32)
        partial_value = partial_value + jnp.dot(flatten_rows(acts_arriving).T, flatten_rows(membrane_arriving), preferred_element_type=jnp.float32)
        rounded = lax.optimization_barrier(partial_value.astype(jnp.bfloat16))
        return running + rounded.astype(jnp.float32)
    gradient = lax.fori_loop(0, N_DP, shard_term, jnp.zeros((FEATURES, FEATURES), jnp.float32))
    fresh_first = FIRST_DECAY * first_old + (1.0 - FIRST_DECAY) * gradient
    fresh_second = SECOND_DECAY * second_old + (1.0 - SECOND_DECAY) * gradient * gradient
    direction = fresh_first / FIRST_CORRECTION / (jnp.sqrt(fresh_second / SECOND_CORRECTION) + EPSILON)
    fresh_params = params - LEARN_RATE * (direction + WEIGHT_DECAY * params)
    product = jnp.dot(upcoming, fresh_params.astype(jnp.bfloat16), preferred_element_type=jnp.float32)
    return (fresh_params, fresh_first, fresh_second, product.astype(jnp.bfloat16))

def reference(master, first_moment, second_moment, inputs_own, inputs_arriving, grads_own, windows_own, windows_arriving, next_inputs):
    outgoing = lax.map(send_grad, (master, grads_own, windows_own))
    received = jnp.concatenate([outgoing[1:], jnp.zeros_like(outgoing[:1])], axis=0)
    fresh_params, fresh_first, fresh_second, next_currents = lax.map(update_section, (master, first_moment, second_moment, inputs_own, inputs_arriving, grads_own, windows_own, received, windows_arriving, next_inputs))
    return (fresh_params, fresh_first, fresh_second, next_currents)
```

```python
import functools

import jax
import jax.numpy as jnp
from jax import lax
from jax.experimental import pallas as pl
from jax.experimental.pallas import tpu as pltpu
from jax.sharding import PartitionSpec as P

LEAK_RATE = 0.5
LEARN_RATE = 0.002
FIRST_DECAY = 0.9
SECOND_DECAY = 0.95
EPSILON = 1e-08
WEIGHT_DECAY = 0.1
FIRST_CORRECTION = 1.0 - 0.9**10
SECOND_CORRECTION = 1.0 - 0.95**10

LANES = 128
PARTS = 8
CHIPS = 4
BF16 = jnp.bfloat16
F32 = jnp.float32


def passed_along(shard, axis, by):
    count = lax.axis_size(axis)
    pairs = [(i, i + by) for i in range(count) if 0 <= i + by < count]
    return lax.ppermute(shard, axis, pairs)


def swapped(shard, bit):
    return lax.ppermute(shard, "dp", [(i, i ^ bit) for i in range(PARTS)])


def over_core(shard):
    return swapped(shard, 1)


def over_x(shard):
    return swapped(shard, 2)


def over_y(shard):
    return swapped(shard, 4)


def cost(flops, *arrays):
    moved = sum(a.size * a.dtype.itemsize for a in arrays)
    return pl.CostEstimate(flops=int(flops), bytes_accessed=int(moved), transcendentals=0)


def adam(params, first, second, gradient):
    fresh_first = FIRST_DECAY * first + (1.0 - FIRST_DECAY) * gradient
    fresh_second = SECOND_DECAY * second + (1.0 - SECOND_DECAY) * gradient * gradient
    direction = (
        fresh_first / FIRST_CORRECTION / (jnp.sqrt(fresh_second / SECOND_CORRECTION) + EPSILON)
    )
    fresh_params = params - LEARN_RATE * (direction + WEIGHT_DECAY * params)
    return fresh_params, fresh_first, fresh_second


def prepare_kernel(where, grads, own, arriving, membrane_t, grads_t, arriving_t):
    steps, rows = grads.shape[0], grads.shape[1]
    window = own[...].T
    arriving_t[...] = arriving[...].T
    carried = jnp.zeros(window.shape, F32)
    for moment in reversed(range(steps)):
        now = grads[moment].astype(F32).T
        lanes = pl.ds(moment * rows, rows)
        grads_t[:, lanes] = now.astype(BF16)
        bit = jnp.bitwise_and(jnp.right_shift(window, moment), 1).astype(F32)
        carried = bit * now + LEAK_RATE * carried
        membrane_t[:, lanes] = carried.astype(BF16)


def prepare(where, grads, own, arriving):
    steps, rows, features = grads.shape
    block = 256
    tokens = steps * rows
    outs = (
        jax.ShapeDtypeStruct((features, tokens), BF16),
        jax.ShapeDtypeStruct((features, tokens), BF16),
        jax.ShapeDtypeStruct((features, rows), jnp.int32),
    )
    return pl.pallas_call(
        prepare_kernel,
        out_shape=outs,
        grid_spec=pltpu.PrefetchScalarGridSpec(
            num_scalar_prefetch=1,
            grid=(features // block,),
            in_specs=[
                pl.BlockSpec((steps, rows, block), lambda i, s: (0, 0, i)),
                pl.BlockSpec((rows, block), lambda i, s: (0, i)),
                pl.BlockSpec((rows, block), lambda i, s: (0, i)),
            ],
            out_specs=[
                pl.BlockSpec((block, tokens), lambda i, s: (i, 0)),
                pl.BlockSpec((block, tokens), lambda i, s: (i, 0)),
                pl.BlockSpec((block, rows), lambda i, s: (i, 0)),
            ],
        ),
        cost_estimate=cost(0, grads, grads, grads, own, arriving, arriving),
        compiler_params=pltpu.CompilerParams(vmem_limit_bytes=16 << 20),
        name="prepare",
    )(where, grads, own, arriving)


def column_block(s, relative, begin, width, rows):
    chip = jnp.bitwise_xor(s[0], relative)
    at = jnp.where(s[1] == 0, begin, 2 * rows - begin - width)
    return (chip * (2 * rows) + at) // width


def through_kernel(splits, pieces, where, *refs):
    weights = refs[: sum(splits)]
    refs = refs[sum(splits) :]
    mine, sibling = refs[:2]
    grads = refs[2 : 2 + 2 * len(pieces)]
    out, total = refs[2 + 2 * len(pieces) :]
    step = pl.program_id(0)
    tokens = mine.shape[1]
    rows = jnp.concatenate([w[...] for w in weights], axis=0)

    @pl.when(step == 0)
    def _():
        total[...] = jnp.zeros_like(total)

    for side, held in enumerate((mine, sibling)):
        lanes = pl.ds(side * tokens, tokens)
        total[:, lanes] += jnp.dot(rows, held[...], preferred_element_type=F32)

    @pl.when(step == pl.num_programs(0) - 1)
    def _():
        at = 0
        for index, (_, _, width) in enumerate(pieces):
            for side in range(2):
                lanes = pl.ds(side * tokens, tokens)
                value = total[pl.ds(at, width), lanes] + grads[2 * index + side][...].astype(F32)
                out[pl.ds(at, width), lanes] = value.astype(BF16)
            at += width


def through(where, pieces, weights, membranes, grads_t, rows):
    features, tokens = membranes[0].shape
    count = sum(p[2] for p in pieces)
    chunk = 512 if features % 512 == 0 else features
    flat = [w for group in weights for w in group]
    out = jax.ShapeDtypeStruct((count, 2 * tokens), BF16)
    specs = [pl.BlockSpec((w.shape[0], chunk), lambda i, s: (0, i)) for w in flat]
    specs += [pl.BlockSpec((chunk, tokens), lambda i, s: (i, 0))] * 2
    grad_operands = []
    for relative, begin, width in pieces:
        for side in range(2):
            specs.append(
                pl.BlockSpec(
                    (width, tokens),
                    functools.partial(
                        lambda i, s, r, b, w: (column_block(s, r, b, w, rows), 0),
                        r=relative,
                        b=begin,
                        w=width,
                    ),
                )
            )
            grad_operands.append(grads_t[side])
    return pl.pallas_call(
        functools.partial(through_kernel, [len(g) for g in weights], pieces),
        out_shape=out,
        grid_spec=pltpu.PrefetchScalarGridSpec(
            num_scalar_prefetch=1,
            grid=(features // chunk,),
            in_specs=specs,
            out_specs=pl.BlockSpec((count, 2 * tokens), lambda i, s: (0, 0)),
            scratch_shapes=[pltpu.VMEM((count, 2 * tokens), F32)],
        ),
        cost_estimate=cost(4 * count * features * tokens, *flat, *membranes, out, out),
        compiler_params=pltpu.CompilerParams(vmem_limit_bytes=24 << 20),
        name="through",
    )(where, *flat, *membranes, *grad_operands)


def partial_kernel(sources, width, where, *refs):
    own = refs[:8]
    windows = refs[8:16]
    arrived = refs[16 : 16 + len(set(a for a, _ in sources))]
    refs = refs[16 + len(arrived) :]
    acts = refs[:4]
    x_keep, x_send, y_keep, y_send, held_own, held_arriving = refs[4:]
    step = pl.program_id(0)
    tokens = own[0].shape[1]
    rows = windows[0].shape[1]

    @pl.when(step == 0)
    def _():
        for chip in range(CHIPS):
            for side in range(2):
                lanes = pl.ds(side * tokens, tokens)
                held_own[pl.ds(chip * width, width), lanes] = own[2 * chip + side][...]
        for relative in range(CHIPS):
            chip = jnp.bitwise_xor(where[0], relative)
            place = pl.ds(pl.multiple_of(chip * width, width), width)
            array, begin = sources[relative]
            for side in range(2):
                window = windows[2 * relative + side][...]
                carried = jnp.zeros(window.shape, F32)
                for moment in reversed(range(tokens // rows)):
                    lanes = pl.ds(side * tokens + moment * rows, rows)
                    now = arrived[array][pl.ds(begin, width), lanes].astype(F32)
                    bit = jnp.bitwise_and(jnp.right_shift(window, moment), 1).astype(F32)
                    carried = bit * now + LEAK_RATE * carried
                    held_arriving[place, lanes] = carried.astype(BF16)

    value = None
    for index, act in enumerate(acts):
        held = (held_own, held_own, held_arriving, held_arriving)[index]
        term = jnp.dot(
            held[:, pl.ds((index % 2) * tokens, tokens)],
            act[...],
            preferred_element_type=F32,
        )
        value = term if value is None else value + term
    value = value.astype(BF16)
    first, last = value[: 2 * width], value[2 * width :]

    @pl.when(jnp.logical_or(step == 0, step == 2))
    def _():
        x_send[0] = first

    @pl.when(jnp.logical_or(step == 1, step == 3))
    def _():
        x_keep[0] = first

    @pl.when(step < 2)
    def _():
        y_send[0] = last

    @pl.when(step >= 2)
    def _():
        y_keep[0] = last


def partials(where, begin, width, membranes, windows_t, arrived, sources, acts, rows):
    features, tokens = membranes[0].shape
    block = 2 * rows
    specs, operands = [], []
    for chip in range(CHIPS):
        for side in range(2):

            def index(i, s, chip=chip):
                return (column_block(s, jnp.bitwise_xor(s[0], chip), begin, width, rows), 0)

            specs.append(pl.BlockSpec((width, tokens), index))
            operands.append(membranes[side])
    for relative in range(CHIPS):
        for side in range(2):
            window = windows_t[side]

            def index(i, s, relative=relative):
                return (column_block(s, relative, begin, width, rows), 0)

            specs.append(pl.BlockSpec((width, window.shape[1]), index))
            operands.append(window)
    for array in arrived:
        specs.append(pl.BlockSpec(array.shape, lambda i, s: (0, 0)))
        operands.append(array)
    for act in acts:
        specs.append(
            pl.BlockSpec((tokens, block), lambda i, s: (0, jnp.bitwise_xor(s[0], 3 - i)))
        )
        operands.append(act)
    piece = jax.ShapeDtypeStruct((2, 2 * width, block), BF16)

    def out_spec(index):
        return pl.BlockSpec((1, 2 * width, block), lambda i, s: (index(i), 0, 0))

    return pl.pallas_call(
        functools.partial(partial_kernel, sources, width),
        out_shape=(piece,) * 4,
        grid_spec=pltpu.PrefetchScalarGridSpec(
            num_scalar_prefetch=1,
            grid=(CHIPS,),
            in_specs=specs,
            out_specs=[
                out_spec(lambda i: jnp.where(i < 3, 1, 0)),
                out_spec(lambda i: jnp.where(i < 2, 1, 0)),
                out_spec(lambda i: jnp.where(i < 3, 1, 0)),
                out_spec(lambda i: jnp.where(i < 1, 1, 0)),
            ],
            scratch_shapes=[pltpu.VMEM((CHIPS * width, 2 * tokens), BF16)] * 2,
        ),
        cost_estimate=cost(32 * width * tokens * features, *acts, piece, piece, piece, piece),
        compiler_params=pltpu.CompilerParams(vmem_limit_bytes=32 << 20),
        name="partials",
    )(where, *operands)


def gather_up_kernel(width, where, xk, xr, xs, yk, yr, ys, mine, other):
    rows = mine.shape[0]
    core = where[1]
    for chip in range(CHIPS):
        kept, received, summed = (xk, xr, xs) if chip < 2 else (yk, yr, ys)
        at = pl.ds((chip % 2) * width, width)
        value = (
            kept[0, at].astype(F32) + received[0, at].astype(F32) + summed[at].astype(F32)
        )
        if width < LANES:
            blank = jnp.zeros((LANES - width, value.shape[1]), F32)
            value = jnp.where(
                core == 0,
                jnp.concatenate([value, blank], axis=0),
                jnp.concatenate([blank, value], axis=0),
            )
        value = value.T.astype(BF16)
        lanes = pl.ds(chip * LANES, LANES)

        @pl.when(core == 0)
        def _(value=value, lanes=lanes):
            mine[:, lanes] = value[:rows]
            other[:, lanes] = value[rows:]

        @pl.when(core != 0)
        def _(value=value, lanes=lanes):
            mine[:, lanes] = value[rows:]
            other[:, lanes] = value[:rows]


def gather_up(where, width, kept_x, got_x, sum_x, kept_y, got_y, sum_y, rows):
    first = pl.BlockSpec((1, 2 * width, 2 * rows), lambda i, s: (0, 0, 0))
    whole = pl.BlockSpec((2 * width, 2 * rows), lambda i, s: (0, 0))
    out = jax.ShapeDtypeStruct((rows, CHIPS * LANES), BF16)
    spec = pl.BlockSpec(out.shape, lambda i, s: (0, 0))
    return pl.pallas_call(
        functools.partial(gather_up_kernel, width),
        out_shape=(out, out),
        grid_spec=pltpu.PrefetchScalarGridSpec(
            num_scalar_prefetch=1,
            grid=(1,),
            in_specs=[first, first, whole, first, first, whole],
            out_specs=[spec, spec],
        ),
        cost_estimate=cost(0, sum_x, sum_x, sum_x, sum_x, sum_x, sum_x, out, out),
        compiler_params=pltpu.CompilerParams(vmem_limit_bytes=24 << 20),
        name="gather_up",
    )(where, kept_x, got_x, sum_x, kept_y, got_y, sum_y)


def update_kernel(whole, where, mine, theirs, params, first, second, acts, *refs):
    fresh_params, fresh_first, fresh_second, currents = refs[-4:]
    if whole:
        own = pl.program_id(1) == where[1]
        gradient = jnp.where(own, mine[...].astype(F32), theirs[...].astype(F32))
    else:
        gradient = mine[...].astype(F32) + theirs[...].astype(F32)
    new = adam(params[...], first[...], second[...], gradient)
    fresh_params[...], fresh_first[...], fresh_second[...] = new
    currents[...] = jnp.dot(
        acts[...], new[0].astype(BF16), preferred_element_type=F32
    ).astype(BF16)


def update(where, begin, width, mine, theirs, state, acts, held):
    params = state[0]
    rows, features = params.shape
    per_chip = 2 * rows // LANES
    whole = width == LANES
    cores = 2 if whole else 1
    tile_of_core = [begin // LANES, (2 * rows - begin - width) // LANES]

    def tile(i, j, s):
        inside = jnp.where(j == 0, tile_of_core[0], tile_of_core[1])
        return (0, per_chip * i + inside)

    block = pl.BlockSpec((rows, LANES), tile)
    grads = pl.BlockSpec((rows, LANES), lambda i, j, s: (0, i))
    current_shape = jax.ShapeDtypeStruct((acts.shape[0], CHIPS * cores * LANES), BF16)
    operands = [where, mine, theirs, *state, acts]
    specs = [grads, grads, block, block, block, pl.BlockSpec(acts.shape, lambda i, j, s: (0, 0))]
    aliases = {}
    if held is not None:
        for index, array in enumerate(held):
            aliases[len(operands)] = index
            operands.append(array)
            specs.append(pl.BlockSpec(memory_space=pl.ANY))
    shape = jax.ShapeDtypeStruct((rows, features), F32)
    *fresh, currents = pl.pallas_call(
        functools.partial(update_kernel, whole),
        out_shape=(shape, shape, shape, current_shape),
        grid_spec=pltpu.PrefetchScalarGridSpec(
            num_scalar_prefetch=1,
            grid=(CHIPS, cores),
            in_specs=specs,
            out_specs=[
                block,
                block,
                block,
                pl.BlockSpec((acts.shape[0], LANES), lambda i, j, s: (0, cores * i + j)),
            ],
        ),
        input_output_aliases=aliases,
        cost_estimate=pl.CostEstimate(
            flops=2 * acts.size * CHIPS * cores * LANES,
            bytes_accessed=24 * rows * CHIPS * cores * LANES,
            transcendentals=0,
        ),
        compiler_params=pltpu.CompilerParams(vmem_limit_bytes=16 << 20),
        name="update",
    )(*operands)
    return fresh, currents


def columns_to_owners(tokens, device):
    count, features = tokens.shape
    width = features // PARTS
    cut = tokens.reshape(count, PARTS, width).transpose(1, 0, 2)
    cut = cut.reshape(2, 2, 2, count, width)
    for axis, bit in ((0, 4), (1, 2), (2, 1)):
        cut = jnp.where(jnp.bitwise_and(device, bit) != 0, jnp.flip(cut, axis), cut)
    held = cut.transpose(2, 0, 1, 3, 4)
    held = jnp.stack([held[0], over_core(held[1])])
    held = held.transpose(2, 0, 1, 3, 4)
    held = jnp.stack([held[0], over_x(held[1])])
    held = held.transpose(3 - 1, 0, 1, 3, 4)
    held = jnp.stack([held[0], over_y(held[1])])
    return held.reshape(PARTS * count, width)


def summed_to_owners(terms):
    rows, columns = terms.shape
    held = terms.reshape(CHIPS, 2, rows // PARTS, columns)

    def add(kept, got):
        return (kept.astype(F32) + got.astype(F32)).astype(BF16)

    held = add(held[:, 0], over_core(held[:, 1]))
    held = held.reshape(2, 2, rows // PARTS, columns)
    held = add(held[:, 0], over_x(held[:, 1]))
    return add(held[0], over_y(held[1]))


def relay_shards(
    master,
    first_moment,
    second_moment,
    inputs_own,
    inputs_arriving,
    grads_own,
    windows_own,
    windows_arriving,
    next_inputs,
):
    params = master[0]
    rows, features = params.shape
    steps, tok_rows = grads_own.shape[1], grads_own.shape[2]
    tokens = steps * tok_rows
    device = lax.axis_index("dp")
    core = jnp.bitwise_and(device, 1)
    where = jnp.stack([device // 2, core]).astype(jnp.int32)

    widths = [LANES] * (rows // LANES) + ([rows % LANES] if rows % LANES else [])
    begins = [sum(widths[:i]) for i in range(len(widths))]
    groups = list(zip(begins, widths))

    held = []
    for begin, width in groups:
        at = jnp.where(core == 0, begin, rows - begin - width)
        held.append(lax.dynamic_slice_in_dim(params, at, width, 0).astype(BF16))
    gathered = []
    for piece in held:
        half = piece.shape[0] // 2
        by_x, by_y = over_x(piece), over_y(piece)
        gathered.append(
            ((by_x,), (by_y,), (over_y(by_x[:half]), over_x(by_y[half:])))
        )

    membrane_t, grads_t, window_t = prepare(
        where, grads_own[0], windows_own[0], windows_arriving[0]
    )
    membranes = (membrane_t, over_core(membrane_t))
    grads_ts = (grads_t, over_core(grads_t))
    acts = []
    for array in (inputs_own, inputs_arriving):
        flat = array[0].reshape(tokens, features)
        acts += [flat, over_core(flat)]
    windows_t = (window_t, over_core(window_t))

    last = len(groups) - 1
    own_pieces = [(0, *groups[g]) for g in range(last)]
    own_arrived = passed_along(
        through(where, own_pieces, [(held[g],) for g in range(last)], membranes, grads_ts, rows),
        "section",
        -1,
    )
    arrived = []
    for g, (begin, width) in enumerate(groups):
        pieces = [(r, begin, width) for r in (1, 2, 3)]
        weights = list(gathered[g])
        if g == last:
            pieces = [(0, begin, width)] + pieces
            weights = [(held[g],)] + weights
        sent = through(where, pieces, weights, membranes, grads_ts, rows)
        got = passed_along(sent, "section", -1)
        if g == last:
            arrived.append(((got,), [(0, r * width) for r in range(CHIPS)]))
        else:
            arrived.append(
                ((own_arrived, got), [(0, begin)] + [(1, r * width) for r in range(3)])
            )

    acts_here = columns_to_owners(next_inputs[0], device)

    fresh = None
    state = (params, first_moment[0], second_moment[0])
    currents = []
    for g, (begin, width) in enumerate(groups):
        x_keep, x_send, y_keep, y_send = partials(
            where, begin, width, membranes, windows_t, *arrived[g], acts, rows
        )
        got_x, got_y = over_x(x_send), over_y(y_send)
        pass_y = (x_keep[1].astype(F32) + got_x[1].astype(F32)).astype(BF16)
        pass_x = (y_keep[1].astype(F32) + got_y[1].astype(F32)).astype(BF16)
        sum_x, sum_y = over_y(pass_y), over_x(pass_x)
        mine, other = gather_up(
            where, width, x_keep, got_x, sum_x, y_keep, got_y, sum_y, rows
        )
        fresh, current = update(
            where, begin, width, mine, over_core(other), state, acts_here, fresh
        )
        currents.append(current)

    early = summed_to_owners(jnp.concatenate(currents[:last], axis=1))
    late = summed_to_owners(currents[last])
    count = early.shape[0]
    tiles = [None] * (2 * rows // LANES)
    for g, (begin, width) in enumerate(groups):
        if g < last:
            size = CHIPS * 2 * LANES
            whole = early[:, g * size : (g + 1) * size].reshape(count, CHIPS, 2, LANES)
            tiles[begin // LANES] = whole[:, :, 0]
            tiles[(2 * rows - begin - width) // LANES] = whole[:, :, 1]
        else:
            tiles[begin // LANES] = late.reshape(count, CHIPS, LANES)
    next_currents = jnp.stack(tiles, axis=2).reshape(count, features)
    return (fresh[0][None], fresh[1][None], fresh[2][None], next_currents[None])


def membrane_grads(gradients, windows):
    carried = jnp.zeros(gradients.shape[1:], F32)
    results = []
    for moment in reversed(range(gradients.shape[0])):
        window = jnp.bitwise_and(jnp.right_shift(windows, moment), 1).astype(F32)
        carried = window * gradients[moment].astype(F32) + LEAK_RATE * carried
        results = [carried] + results
    return jnp.stack(results).astype(BF16)


def plain_shards(
    master,
    first_moment,
    second_moment,
    inputs_own,
    inputs_arriving,
    grads_own,
    windows_own,
    windows_arriving,
    next_inputs,
):
    params = master[0]
    timesteps, tok_rows, features = (grads_own.shape[1], grads_own.shape[2], grads_own.shape[3])
    flat_rows = timesteps * tok_rows
    membrane_own = membrane_grads(grads_own[0], windows_own[0]).reshape(flat_rows, features)
    weights = lax.all_gather(params.astype(BF16), "dp", axis=0, tiled=True)
    across = (((1,), (1,)), ((), ()))
    product = lax.dot_general(membrane_own, weights, across, preferred_element_type=F32)
    summed = grads_own[0].reshape(flat_rows, features).astype(F32) + product
    outgoing = summed.astype(BF16).reshape(timesteps, tok_rows, features)
    received = passed_along(outgoing, "section", -1)
    membrane_arriving = membrane_grads(received, windows_arriving[0]).reshape(flat_rows, features)
    contract = (((0,), (0,)), ((), ()))
    partial_value = lax.dot_general(
        inputs_own[0].reshape(flat_rows, features),
        membrane_own,
        contract,
        preferred_element_type=F32,
    ) + lax.dot_general(
        inputs_arriving[0].reshape(flat_rows, features),
        membrane_arriving,
        contract,
        preferred_element_type=F32,
    )
    gradient = lax.psum_scatter(
        partial_value.astype(BF16), "dp", scatter_dimension=0, tiled=True
    ).astype(F32)
    fresh_params, fresh_first, fresh_second = adam(
        params, first_moment[0], second_moment[0], gradient
    )
    gathered = lax.all_gather(fresh_params.astype(BF16), "dp", axis=0, tiled=True)
    currents = jnp.dot(next_inputs[0], gathered, preferred_element_type=F32)
    return (
        fresh_params[None],
        fresh_first[None],
        fresh_second[None],
        currents.astype(BF16)[None],
    )


def solution(mesh):
    rows = P("section", "dp", None)
    acts = P("section", None, "dp", None)
    return jax.shard_map(
        relay_shards if mesh.shape["dp"] == PARTS else plain_shards,
        mesh=mesh,
        in_specs=(rows, rows, rows, acts, acts, acts, rows, rows, rows),
        out_specs=(rows, rows, rows, rows),
        check_vma=False,
    )
```

```python
import functools

import jax
import jax.numpy as jnp
from jax import lax
from jax.experimental import pallas as pl
from jax.experimental.pallas import tpu as pltpu
from jax.sharding import PartitionSpec as P

LEAK_RATE = 0.5
LEARN_RATE = 0.002
FIRST_DECAY = 0.9
SECOND_DECAY = 0.95
EPSILON = 1e-08
WEIGHT_DECAY = 0.1
FIRST_CORRECTION = 1.0 - 0.9**10
SECOND_CORRECTION = 1.0 - 0.95**10

LANES = 128
PARTS = 8
CHIPS = 4
BF16 = jnp.bfloat16
F32 = jnp.float32


def passed_along(shard, axis, by):
    count = lax.axis_size(axis)
    pairs = [(i, i + by) for i in range(count) if 0 <= i + by < count]
    return lax.ppermute(shard, axis, pairs)


def swapped(shard, bit):
    return lax.ppermute(shard, "dp", [(i, i ^ bit) for i in range(PARTS)])


def over_core(shard):
    return swapped(shard, 1)


def over_x(shard):
    return swapped(shard, 2)


def over_y(shard):
    return swapped(shard, 4)


def tied(held, *earlier):
    return lax.optimization_barrier((held, *earlier))[0]


SMALL = pl.CostEstimate(flops=1, bytes_accessed=1, transcendentals=0)
VMEM = 60 << 20


def adam(params, first, second, gradient):
    fresh_first = FIRST_DECAY * first + (1.0 - FIRST_DECAY) * gradient
    fresh_second = SECOND_DECAY * second + (1.0 - SECOND_DECAY) * gradient * gradient
    direction = (
        fresh_first / FIRST_CORRECTION / (jnp.sqrt(fresh_second / SECOND_CORRECTION) + EPSILON)
    )
    fresh_params = params - LEARN_RATE * (direction + WEIGHT_DECAY * params)
    return fresh_params, fresh_first, fresh_second


def prepare_kernel(groups, where, *refs):
    grads, own, arriving = refs[0:2], refs[2:4], refs[4:6]
    membrane_t, grads_t, window_t = refs[6:]
    steps, tok_rows = grads[0].shape[0], grads[0].shape[1]
    rows = own[0].shape[1] // 2
    chip = pl.program_id(0)
    for side in range(2):
        window = own[side][...].T
        later = arriving[side][...].T
        carried = jnp.zeros(window.shape, F32)
        values = []
        for moment in reversed(range(steps)):
            now = grads[side][moment].astype(F32).T
            bit = jnp.bitwise_and(jnp.right_shift(window, moment), 1).astype(F32)
            carried = bit * now + LEAK_RATE * carried
            lanes = pl.ds((side * steps + moment) * tok_rows, tok_rows)
            membrane_t[:, lanes] = carried.astype(BF16)
            values.append((lanes, now.astype(BF16)))
        for core in range(2):

            @pl.when(where[1] == core)
            def _(core=core, later=later, values=values, side=side):
                for begin, width in groups:
                    at = begin if core == 0 else 2 * rows - begin - width
                    place = pl.ds(pl.multiple_of(CHIPS * begin + chip * width, width), width)
                    window_t[place, pl.ds(side * tok_rows, tok_rows)] = later[at : at + width]
                    for lanes, value in values:
                        grads_t[place, lanes] = value[at : at + width]


def prepare(where, grads, own, arriving, groups, rows):
    steps, tok_rows, features = grads[0].shape
    block = 2 * rows
    tokens = 2 * steps * tok_rows
    cut = CHIPS * rows
    outs = (
        jax.ShapeDtypeStruct((features, tokens), BF16),
        jax.ShapeDtypeStruct((cut, tokens), BF16),
        jax.ShapeDtypeStruct((cut, 2 * tok_rows), jnp.int32),
    )
    whole = [pl.BlockSpec(o.shape, lambda i, s: (0, 0)) for o in outs[1:]]
    return pl.pallas_call(
        functools.partial(prepare_kernel, groups),
        out_shape=outs,
        grid_spec=pltpu.PrefetchScalarGridSpec(
            num_scalar_prefetch=1,
            grid=(features // block,),
            in_specs=[pl.BlockSpec((steps, tok_rows, block), lambda i, s: (0, 0, i))] * 2
            + [pl.BlockSpec((tok_rows, block), lambda i, s: (0, i))] * 4,
            out_specs=[pl.BlockSpec((block, tokens), lambda i, s: (i, 0)), *whole],
        ),
        cost_estimate=SMALL,
        compiler_params=pltpu.CompilerParams(vmem_limit_bytes=VMEM),
        name="prepare",
    )(where, *grads, *own, *arriving)


def compact_block(s, relative, begin, width):
    return CHIPS * begin // width + jnp.bitwise_xor(s[0], relative)


def column_block(s, relative, begin, width, rows):
    chip = jnp.bitwise_xor(s[0], relative)
    at = jnp.where(s[1] == 0, begin, 2 * rows - begin - width)
    return (chip * (2 * rows) + at) // width


def through_kernel(count, pieces, where, *refs):
    weights, held = refs[:count], refs[count]
    grads = refs[count + 1 : count + 1 + len(pieces)]
    out, total = refs[count + 1 + len(pieces) :]
    step = pl.program_id(0)
    rows = jnp.concatenate([w[...] for w in weights], axis=0)
    half = held.shape[1] // 2
    for side in range(2):
        lanes = pl.ds(side * half, half)
        term = jnp.dot(rows, held[:, lanes], preferred_element_type=F32)

        @pl.when(step == 0)
        def _(lanes=lanes, term=term):
            total[:, lanes] = term

        @pl.when(step != 0)
        def _(lanes=lanes, term=term):
            at = 0
            for (_, _, width), grad in zip(pieces, grads):
                value = total[pl.ds(at, width), lanes] + term[at : at + width]
                out[pl.ds(at, width), lanes] = (value + grad[:, lanes].astype(F32)).astype(BF16)
                at += width


def through(where, pieces, weights, membrane_t, grads_t):
    features, tokens = membrane_t.shape
    count = sum(p[2] for p in pieces)
    chunk = features // 2
    out = jax.ShapeDtypeStruct((count, tokens), BF16)
    specs = [pl.BlockSpec((w.shape[0], chunk), lambda i, s: (0, i)) for w in weights]
    specs.append(pl.BlockSpec((chunk, tokens), lambda i, s: (i, 0)))
    for relative, begin, width in pieces:
        specs.append(
            pl.BlockSpec(
                (width, tokens),
                functools.partial(
                    lambda i, s, r, b, w: (compact_block(s, r, b, w), 0), r=relative, b=begin, w=width
                ),
            )
        )
    return pl.pallas_call(
        functools.partial(through_kernel, len(weights), pieces),
        out_shape=out,
        grid_spec=pltpu.PrefetchScalarGridSpec(
            num_scalar_prefetch=1,
            grid=(2,),
            in_specs=specs,
            out_specs=pl.BlockSpec((count, tokens), lambda i, s: (0, 0)),
            scratch_shapes=[pltpu.VMEM((count, tokens), F32)],
        ),
        cost_estimate=SMALL,
        compiler_params=pltpu.CompilerParams(vmem_limit_bytes=VMEM),
        name="through",
    )(where, *weights, membrane_t, *([grads_t] * len(pieces)))


def partial_kernel(sources, count, width, where, *refs):
    own, windows = refs[:CHIPS], refs[CHIPS : 2 * CHIPS]
    arrived = refs[2 * CHIPS : 2 * CHIPS + count]
    refs = refs[2 * CHIPS + count :]
    acts = refs[:4]
    x_keep, x_send, y_keep, y_send, held = refs[4:]
    step = pl.program_id(0)
    tokens = own[0].shape[1]
    rows = windows[0].shape[1] // 2
    moments = tokens // (2 * rows)

    @pl.when(step == 0)
    def _():
        for chip in range(CHIPS):
            held[pl.ds(chip * width, width), :tokens] = own[chip][...]
        for relative in range(CHIPS):
            chip = jnp.bitwise_xor(where[0], relative)
            place = pl.ds(pl.multiple_of(chip * width, width), width)
            array, begin = sources[relative]
            for side in range(2):
                window = windows[relative][:, side * rows : (side + 1) * rows]
                carried = jnp.zeros(window.shape, F32)
                for moment in reversed(range(moments)):
                    at = (side * moments + moment) * rows
                    now = arrived[array][pl.ds(begin, width), pl.ds(at, rows)].astype(F32)
                    bit = jnp.bitwise_and(jnp.right_shift(window, moment), 1).astype(F32)
                    carried = bit * now + LEAK_RATE * carried
                    held[place, pl.ds(tokens + at, rows)] = carried.astype(BF16)

    value = None
    for index, act in enumerate(acts):
        term = lax.dot_general(
            act[...],
            held[:, pl.ds(index * tokens // 2, tokens // 2)],
            (((0,), (1,)), ((), ())),
            preferred_element_type=F32,
        )
        value = term if value is None else value + term
    value = value.astype(BF16)
    first, last = value[:, : 2 * width], value[:, 2 * width :]

    @pl.when(jnp.logical_or(step == 0, step == 2))
    def _():
        x_send[0] = first

    @pl.when(jnp.logical_or(step == 1, step == 3))
    def _():
        x_keep[0] = first

    @pl.when(step < 2)
    def _():
        y_send[0] = last

    @pl.when(step >= 2)
    def _():
        y_keep[0] = last


def partials(where, begin, width, membrane_t, window_t, arrived, sources, acts, rows):
    tokens = membrane_t.shape[1]
    block = 2 * rows
    specs, operands = [], []
    for chip in range(CHIPS):

        def index(i, s, chip=chip):
            return (column_block(s, jnp.bitwise_xor(s[0], chip), begin, width, rows), 0)

        specs.append(pl.BlockSpec((width, tokens), index))
        operands.append(membrane_t)
    for relative in range(CHIPS):

        def index(i, s, relative=relative):
            return (compact_block(s, relative, begin, width), 0)

        specs.append(pl.BlockSpec((width, window_t.shape[1]), index))
        operands.append(window_t)
    for array in arrived:
        specs.append(pl.BlockSpec(array.shape, lambda i, s: (0, 0)))
        operands.append(array)
    for act in acts:
        specs.append(
            pl.BlockSpec((act.shape[0], block), lambda i, s: (0, jnp.bitwise_xor(s[0], 3 - i)))
        )
        operands.append(act)
    piece = jax.ShapeDtypeStruct((2, block, 2 * width), BF16)

    def out_spec(index):
        return pl.BlockSpec((1, block, 2 * width), lambda i, s: (index(i), 0, 0))

    return pl.pallas_call(
        functools.partial(partial_kernel, sources, len(arrived), width),
        out_shape=(piece,) * 4,
        grid_spec=pltpu.PrefetchScalarGridSpec(
            num_scalar_prefetch=1,
            grid=(CHIPS,),
            in_specs=specs,
            out_specs=[
                out_spec(lambda i: jnp.where(i < 3, 1, 0)),
                out_spec(lambda i: jnp.where(i < 2, 1, 0)),
                out_spec(lambda i: jnp.where(i < 3, 1, 0)),
                out_spec(lambda i: jnp.where(i < 1, 1, 0)),
            ],
            scratch_shapes=[pltpu.VMEM((CHIPS * width, 2 * tokens), BF16)],
        ),
        cost_estimate=SMALL,
        compiler_params=pltpu.CompilerParams(vmem_limit_bytes=28 << 20),
        name="partials",
    )(where, *operands)


def gather_up_kernel(width, where, xk, xr, xs, yk, yr, ys, mine, other):
    rows = mine.shape[0]
    parts = []
    for kept, received, summed in ((xk, xr, xs), (yk, yr, ys)):
        value = kept[0].astype(F32) + received[0].astype(F32) + summed[...].astype(F32)
        parts.append(value.astype(BF16))
    value = jnp.concatenate(parts, axis=1)
    if width < LANES:
        pieces = [value[:, chip * width : (chip + 1) * width] for chip in range(CHIPS)]
        blank = jnp.zeros((value.shape[0], LANES - width), BF16)
        low = jnp.concatenate([p for piece in pieces for p in (piece, blank)], axis=1)
        high = jnp.concatenate([p for piece in pieces for p in (blank, piece)], axis=1)
        value = jnp.where(where[1] == 0, low.astype(F32), high.astype(F32)).astype(BF16)

    @pl.when(where[1] == 0)
    def _():
        mine[...] = value[:rows]
        other[...] = value[rows:]

    @pl.when(where[1] != 0)
    def _():
        mine[...] = value[rows:]
        other[...] = value[:rows]


def gather_up(where, width, kept_x, got_x, sum_x, kept_y, got_y, sum_y, rows):
    first = pl.BlockSpec((1, 2 * rows, 2 * width), lambda i, s: (0, 0, 0))
    whole = pl.BlockSpec((2 * rows, 2 * width), lambda i, s: (0, 0))
    out = jax.ShapeDtypeStruct((rows, CHIPS * LANES), BF16)
    spec = pl.BlockSpec(out.shape, lambda i, s: (0, 0))
    return pl.pallas_call(
        functools.partial(gather_up_kernel, width),
        out_shape=(out, out),
        grid_spec=pltpu.PrefetchScalarGridSpec(
            num_scalar_prefetch=1,
            grid=(1,),
            in_specs=[first, first, whole, first, first, whole],
            out_specs=[spec, spec],
        ),
        cost_estimate=SMALL,
        compiler_params=pltpu.CompilerParams(vmem_limit_bytes=12 << 20),
        name="gather_up",
    )(where, kept_x, got_x, sum_x, kept_y, got_y, sum_y)


def update_kernel(whole, where, mine, theirs, params, first, second, acts, *refs):
    fresh_params, fresh_first, fresh_second, currents = refs[-4:]
    if whole:
        own = pl.program_id(1) == where[1]
        gradient = jnp.where(own, mine[...].astype(F32), theirs[...].astype(F32))
    else:
        gradient = mine[...].astype(F32) + theirs[...].astype(F32)
    new = adam(params[...], first[...], second[...], gradient)
    fresh_params[...], fresh_first[...], fresh_second[...] = new
    currents[...] = jnp.dot(
        acts[...], new[0].astype(BF16), preferred_element_type=F32
    ).astype(BF16)


def update(where, begin, width, mine, theirs, state, acts, held):
    params = state[0]
    rows, features = params.shape
    per_chip = 2 * rows // LANES
    whole = width == LANES
    cores = 2 if whole else 1
    tile_of_core = [begin // LANES, (2 * rows - begin - width) // LANES]

    def tile(i, j, s):
        inside = jnp.where(j == 0, tile_of_core[0], tile_of_core[1])
        return (0, per_chip * i + inside)

    block = pl.BlockSpec((rows, LANES), tile)
    grads = pl.BlockSpec((rows, LANES), lambda i, j, s: (0, i))
    current_shape = jax.ShapeDtypeStruct((acts.shape[0], CHIPS * cores * LANES), BF16)
    operands = [where, mine, theirs, *state, acts]
    specs = [grads, grads, block, block, block, pl.BlockSpec(acts.shape, lambda i, j, s: (0, 0))]
    aliases = {}
    if held is not None:
        for index, array in enumerate(held):
            aliases[len(operands)] = index
            operands.append(array)
            specs.append(pl.BlockSpec(memory_space=pl.ANY))
    shape = jax.ShapeDtypeStruct((rows, features), F32)
    *fresh, currents = pl.pallas_call(
        functools.partial(update_kernel, whole),
        out_shape=(shape, shape, shape, current_shape),
        grid_spec=pltpu.PrefetchScalarGridSpec(
            num_scalar_prefetch=1,
            grid=(CHIPS, cores),
            in_specs=specs,
            out_specs=[
                block,
                block,
                block,
                pl.BlockSpec((acts.shape[0], LANES), lambda i, j, s: (0, cores * i + j)),
            ],
        ),
        input_output_aliases=aliases,
        cost_estimate=pl.CostEstimate(
            flops=2 * acts.size * CHIPS * cores * LANES,
            bytes_accessed=24 * rows * CHIPS * cores * LANES,
            transcendentals=0,
        ),
        compiler_params=pltpu.CompilerParams(vmem_limit_bytes=8 << 20),
        name="update",
    )(*operands)
    return fresh, currents


def columns_to_owners(tokens, device):
    count, features = tokens.shape
    width = features // PARTS
    cut = tokens.reshape(count, PARTS, width).transpose(1, 0, 2)
    cut = cut.reshape(2, 2, 2, count, width)
    for axis, bit in ((0, 4), (1, 2), (2, 1)):
        cut = jnp.where(jnp.bitwise_and(device, bit) != 0, jnp.flip(cut, axis), cut)
    held = cut.transpose(2, 0, 1, 3, 4)
    held = jnp.stack([held[0], over_core(held[1])])
    held = held.transpose(2, 0, 1, 3, 4)
    held = jnp.stack([held[0], over_x(held[1])])
    held = held.transpose(3 - 1, 0, 1, 3, 4)
    held = jnp.stack([held[0], over_y(held[1])])
    return held.reshape(PARTS * count, width)


def summed_to_owners(terms):
    rows, columns = terms.shape
    held = terms.reshape(CHIPS, 2, rows // PARTS, columns)

    def add(kept, got):
        return (kept.astype(F32) + got.astype(F32)).astype(BF16)

    held = add(held[:, 0], over_core(held[:, 1]))
    held = held.reshape(2, 2, rows // PARTS, columns)
    held = add(held[:, 0], over_x(held[:, 1]))
    return add(held[0], over_y(held[1]))


def relay_shards(
    master,
    first_moment,
    second_moment,
    inputs_own,
    inputs_arriving,
    grads_own,
    windows_own,
    windows_arriving,
    next_inputs,
):
    params = master[0]
    rows, features = params.shape
    steps, tok_rows = grads_own.shape[1], grads_own.shape[2]
    tokens = steps * tok_rows
    device = lax.axis_index("dp")
    core = jnp.bitwise_and(device, 1)
    where = jnp.stack([device // 2, core]).astype(jnp.int32)

    widths = [LANES] * (rows // LANES) + ([rows % LANES] if rows % LANES else [])
    begins = [sum(widths[:i]) for i in range(len(widths))]
    groups = list(zip(begins, widths))

    held = []
    for begin, width in groups:
        at = jnp.where(core == 0, begin, rows - begin - width)
        source = params if not held else tied(params, held[0])
        held.append(lax.dynamic_slice_in_dim(source, at, width, 0).astype(BF16))

    def forward(by_x, by_y, *after):
        half = by_x.shape[0] // 2
        first, second = by_x[:half], by_y[half:]
        if after:
            first, second = tied(first, *after), tied(second, *after)
        return over_y(first), over_x(second)

    x0, y0 = over_x(held[0]), over_y(held[0])
    both = []
    for array in (grads_own, windows_own, windows_arriving):
        both.append((array[0], over_core(array[0])))
    piece = tied(held[1], both[0][1])
    x1, y1 = over_x(piece), over_y(piece)
    membrane_t, grads_t, window_t = prepare(where, *both, groups, rows)
    d0 = forward(x0, y0, membrane_t)

    (b0, w0), (b1, w1), (b2, w2) = groups

    def send(pieces, weights):
        sent = through(where, pieces, weights, membrane_t, grads_t)
        return sent, passed_along(sent, "section", -1)

    sent_a, got_a = send(
        [(0, b0, w0), (0, b1, w1), (1, b0, w0), (2, b0, w0)], [held[0], held[1], x0, y0]
    )
    piece = tied(held[2], x1, y1, sent_a)
    x2, y2 = over_x(piece), over_y(piece)
    acts = []
    for array in (inputs_own, inputs_arriving):
        flat = array[0].reshape(tokens, features)
        acts += [flat, over_core(tied(flat, x2, y2))]
    sent_b, got_b = send(
        [(3, b0, w0), (1, b1, w1), (2, b1, w1)], [*d0, x1, y1]
    )
    d1 = forward(x1, y1, sent_a)
    d2 = forward(x2, y2, sent_b)
    sent_c, got_c = send(
        [(3, b1, w1), (0, b2, w2), (1, b2, w2), (2, b2, w2), (3, b2, w2)],
        [*d1, held[2], tied(x2, got_a), y2, *d2],
    )

    def sum_up(g, arrived, sources, *after):
        begin, width = groups[g]
        if after:
            arrived = tied(arrived, *after)
        return partials(
            where, begin, width, membrane_t, window_t, arrived, sources, acts, rows
        )

    def first_stage(pieces):
        return over_x(pieces[1]), over_y(pieces[3])

    def second_stage(pieces, got):
        pass_y = (pieces[0][1].astype(F32) + got[0][1].astype(F32)).astype(BF16)
        pass_x = (pieces[2][1].astype(F32) + got[1][1].astype(F32)).astype(BF16)
        return over_y(pass_y), over_x(pass_x), (pass_y, pass_x)

    state = (params, first_moment[0], second_moment[0])

    def finish(g, pieces, got, sums, fresh, *after):
        begin, width = groups[g]
        sum_x = tied(sums[0], *after) if after else sums[0]
        mine, other = gather_up(
            where, width, pieces[0], got[0], sum_x, pieces[2], got[1], sums[1], rows
        )
        return update(where, begin, width, mine, over_core(other), state, acts_here, fresh)

    pieces0 = sum_up(
        0, (got_a, got_b), [(0, 0), (0, w0 + w1), (0, 2 * w0 + w1), (1, 0)], sent_c
    )
    got0 = first_stage(pieces0)
    acts_here = columns_to_owners(tied(next_inputs[0], sent_c), device)
    pieces1 = sum_up(
        1, (got_a, got_b, got_c), [(0, w0), (1, w0), (1, w0 + w1), (2, 0)], pieces0[0]
    )
    got1 = first_stage(pieces1)
    sums0 = second_stage(pieces0, got0)
    pieces2 = sum_up(
        2, (got_c,), [(0, w1 + r * w2) for r in range(CHIPS)], pieces1[0], *sums0[2]
    )
    got2 = first_stage(pieces2)
    sums1 = second_stage(pieces1, got1)
    fresh, current0 = finish(0, pieces0, got0, sums0, None, pieces2[0])
    sums2 = second_stage(pieces2, got2)
    fresh, current1 = finish(1, pieces1, got1, sums1, fresh)
    fresh, current2 = finish(2, pieces2, got2, sums2, fresh, current1)
    last = len(groups) - 1
    currents = [current0, current1, current2]

    early = summed_to_owners(jnp.concatenate(currents[:last], axis=1))
    late = summed_to_owners(currents[last])
    count = early.shape[0]
    tiles = [None] * (2 * rows // LANES)
    for g, (begin, width) in enumerate(groups):
        if g < last:
            size = CHIPS * 2 * LANES
            whole = early[:, g * size : (g + 1) * size].reshape(count, CHIPS, 2, LANES)
            tiles[begin // LANES] = whole[:, :, 0]
            tiles[(2 * rows - begin - width) // LANES] = whole[:, :, 1]
        else:
            tiles[begin // LANES] = late.reshape(count, CHIPS, LANES)
    next_currents = jnp.stack(tiles, axis=2).reshape(count, features)
    return (fresh[0][None], fresh[1][None], fresh[2][None], next_currents[None])


def membrane_grads(gradients, windows):
    carried = jnp.zeros(gradients.shape[1:], F32)
    results = []
    for moment in reversed(range(gradients.shape[0])):
        window = jnp.bitwise_and(jnp.right_shift(windows, moment), 1).astype(F32)
        carried = window * gradients[moment].astype(F32) + LEAK_RATE * carried
        results = [carried] + results
    return jnp.stack(results).astype(BF16)


def plain_shards(
    master,
    first_moment,
    second_moment,
    inputs_own,
    inputs_arriving,
    grads_own,
    windows_own,
    windows_arriving,
    next_inputs,
):
    params = master[0]
    timesteps, tok_rows, features = (grads_own.shape[1], grads_own.shape[2], grads_own.shape[3])
    flat_rows = timesteps * tok_rows
    membrane_own = membrane_grads(grads_own[0], windows_own[0]).reshape(flat_rows, features)
    weights = lax.all_gather(params.astype(BF16), "dp", axis=0, tiled=True)
    across = (((1,), (1,)), ((), ()))
    product = lax.dot_general(membrane_own, weights, across, preferred_element_type=F32)
    summed = grads_own[0].reshape(flat_rows, features).astype(F32) + product
    outgoing = summed.astype(BF16).reshape(timesteps, tok_rows, features)
    received = passed_along(outgoing, "section", -1)
    membrane_arriving = membrane_grads(received, windows_arriving[0]).reshape(flat_rows, features)
    contract = (((0,), (0,)), ((), ()))
    partial_value = lax.dot_general(
        inputs_own[0].reshape(flat_rows, features),
        membrane_own,
        contract,
        preferred_element_type=F32,
    ) + lax.dot_general(
        inputs_arriving[0].reshape(flat_rows, features),
        membrane_arriving,
        contract,
        preferred_element_type=F32,
    )
    gradient = lax.psum_scatter(
        partial_value.astype(BF16), "dp", scatter_dimension=0, tiled=True
    ).astype(F32)
    fresh_params, fresh_first, fresh_second = adam(
        params, first_moment[0], second_moment[0], gradient
    )
    gathered = lax.all_gather(fresh_params.astype(BF16), "dp", axis=0, tiled=True)
    currents = jnp.dot(next_inputs[0], gathered, preferred_element_type=F32)
    return (
        fresh_params[None],
        fresh_first[None],
        fresh_second[None],
        currents.astype(BF16)[None],
    )


def solution(mesh):
    rows = P("section", "dp", None)
    acts = P("section", None, "dp", None)
    return jax.shard_map(
        relay_shards if mesh.shape["dp"] == PARTS else plain_shards,
        mesh=mesh,
        in_specs=(rows, rows, rows, acts, acts, acts, rows, rows, rows),
        out_specs=(rows, rows, rows, rows),
        check_vma=False,
    )
```

```python
import functools

import jax
import jax.numpy as jnp
from jax import lax
from jax.experimental import pallas as pl
from jax.experimental.pallas import tpu as pltpu
from jax.sharding import PartitionSpec as P

LEAK_RATE = 0.5
LEARN_RATE = 0.002
FIRST_DECAY = 0.9
SECOND_DECAY = 0.95
EPSILON = 1e-08
WEIGHT_DECAY = 0.1
FIRST_CORRECTION = 1.0 - 0.9**10
SECOND_CORRECTION = 1.0 - 0.95**10

LANES = 128
PARTS = 8
CHIPS = 4
BF16 = jnp.bfloat16
F32 = jnp.float32


def passed_along(shard, axis, by):
    count = lax.axis_size(axis)
    pairs = [(i, i + by) for i in range(count) if 0 <= i + by < count]
    return lax.ppermute(shard, axis, pairs)


def swapped(shard, bit):
    return lax.ppermute(shard, "dp", [(i, i ^ bit) for i in range(PARTS)])


def over_core(shard):
    return swapped(shard, 1)


def over_x(shard):
    return swapped(shard, 2)


def over_y(shard):
    return swapped(shard, 4)


def tied(held, *earlier):
    return lax.optimization_barrier((held, *earlier))[0]


SMALL = pl.CostEstimate(flops=10**10, bytes_accessed=10**7, transcendentals=0)
VMEM = 60 << 20


def adam(params, first, second, gradient):
    fresh_first = FIRST_DECAY * first + (1.0 - FIRST_DECAY) * gradient
    fresh_second = SECOND_DECAY * second + (1.0 - SECOND_DECAY) * gradient * gradient
    direction = (
        fresh_first / FIRST_CORRECTION / (jnp.sqrt(fresh_second / SECOND_CORRECTION) + EPSILON)
    )
    fresh_params = params - LEARN_RATE * (direction + WEIGHT_DECAY * params)
    return fresh_params, fresh_first, fresh_second


def prepare_kernel(groups, where, *refs):
    grads, own, arriving = refs[0:2], refs[2:4], refs[4:6]
    membrane_t, grads_t, window_t = refs[6:]
    steps, tok_rows = grads[0].shape[0], grads[0].shape[1]
    rows = own[0].shape[1] // 2
    chip = pl.program_id(0)
    for side in range(2):
        window = own[side][...].T
        later = arriving[side][...].T
        carried = jnp.zeros(window.shape, F32)
        values = []
        for moment in reversed(range(steps)):
            now = grads[side][moment].astype(F32).T
            bit = jnp.bitwise_and(jnp.right_shift(window, moment), 1).astype(F32)
            carried = bit * now + LEAK_RATE * carried
            lanes = pl.ds((side * steps + moment) * tok_rows, tok_rows)
            membrane_t[:, lanes] = carried.astype(BF16)
            values.append((lanes, now.astype(BF16)))
        for core in range(2):

            @pl.when(where[1] == core)
            def _(core=core, later=later, values=values, side=side):
                for begin, width in groups:
                    at = begin if core == 0 else 2 * rows - begin - width
                    place = pl.ds(pl.multiple_of(CHIPS * begin + chip * width, width), width)
                    window_t[place, pl.ds(side * tok_rows, tok_rows)] = later[at : at + width]
                    for lanes, value in values:
                        grads_t[place, lanes] = value[at : at + width]


def prepare(where, grads, own, arriving, groups, rows):
    steps, tok_rows, features = grads[0].shape
    block = 2 * rows
    tokens = 2 * steps * tok_rows
    cut = CHIPS * rows
    outs = (
        jax.ShapeDtypeStruct((features, tokens), BF16),
        jax.ShapeDtypeStruct((cut, tokens), BF16),
        jax.ShapeDtypeStruct((cut, 2 * tok_rows), jnp.int32),
    )
    whole = [pl.BlockSpec(o.shape, lambda i, s: (0, 0)) for o in outs[1:]]
    return pl.pallas_call(
        functools.partial(prepare_kernel, groups),
        out_shape=outs,
        grid_spec=pltpu.PrefetchScalarGridSpec(
            num_scalar_prefetch=1,
            grid=(features // block,),
            in_specs=[pl.BlockSpec((steps, tok_rows, block), lambda i, s: (0, 0, i))] * 2
            + [pl.BlockSpec((tok_rows, block), lambda i, s: (0, i))] * 4,
            out_specs=[pl.BlockSpec((block, tokens), lambda i, s: (i, 0)), *whole],
        ),
        cost_estimate=SMALL,
        compiler_params=pltpu.CompilerParams(vmem_limit_bytes=VMEM),
        name="prepare",
    )(where, *grads, *own, *arriving)


def compact_block(s, relative, begin, width):
    return CHIPS * begin // width + jnp.bitwise_xor(s[0], relative)


def column_block(s, relative, begin, width, rows):
    chip = jnp.bitwise_xor(s[0], relative)
    at = jnp.where(s[1] == 0, begin, 2 * rows - begin - width)
    return (chip * (2 * rows) + at) // width


def through_kernel(count, pieces, where, *refs):
    weights, held = refs[:count], refs[count]
    grads = refs[count + 1 : count + 1 + len(pieces)]
    out, total = refs[count + 1 + len(pieces) :]
    step = pl.program_id(0)
    rows = jnp.concatenate([w[...] for w in weights], axis=0)
    half = held.shape[1] // 2
    for side in range(2):
        lanes = pl.ds(side * half, half)
        term = jnp.dot(rows, held[:, lanes], preferred_element_type=F32)

        @pl.when(step == 0)
        def _(lanes=lanes, term=term):
            total[:, lanes] = term

        @pl.when(step != 0)
        def _(lanes=lanes, term=term):
            at = 0
            for (_, _, width), grad in zip(pieces, grads):
                value = total[pl.ds(at, width), lanes] + term[at : at + width]
                out[pl.ds(at, width), lanes] = (value + grad[:, lanes].astype(F32)).astype(BF16)
                at += width


def through(where, pieces, weights, membrane_t, grads_t):
    features, tokens = membrane_t.shape
    count = sum(p[2] for p in pieces)
    chunk = features // 2
    out = jax.ShapeDtypeStruct((count, tokens), BF16)
    specs = [pl.BlockSpec((w.shape[0], chunk), lambda i, s: (0, i)) for w in weights]
    specs.append(pl.BlockSpec((chunk, tokens), lambda i, s: (i, 0)))
    for relative, begin, width in pieces:
        specs.append(
            pl.BlockSpec(
                (width, tokens),
                functools.partial(
                    lambda i, s, r, b, w: (compact_block(s, r, b, w), 0), r=relative, b=begin, w=width
                ),
            )
        )
    return pl.pallas_call(
        functools.partial(through_kernel, len(weights), pieces),
        out_shape=out,
        grid_spec=pltpu.PrefetchScalarGridSpec(
            num_scalar_prefetch=1,
            grid=(2,),
            in_specs=specs,
            out_specs=pl.BlockSpec((count, tokens), lambda i, s: (0, 0)),
            scratch_shapes=[pltpu.VMEM((count, tokens), F32)],
        ),
        cost_estimate=SMALL,
        compiler_params=pltpu.CompilerParams(vmem_limit_bytes=VMEM),
        name="through",
    )(where, *weights, membrane_t, *([grads_t] * len(pieces)))


def partial_kernel(sources, count, width, where, *refs):
    own, windows = refs[:CHIPS], refs[CHIPS : 2 * CHIPS]
    arrived = refs[2 * CHIPS : 2 * CHIPS + count]
    refs = refs[2 * CHIPS + count :]
    acts = refs[:4]
    x_keep, x_send, y_keep, y_send, held = refs[4:]
    step = pl.program_id(0)
    tokens = own[0].shape[1]
    rows = windows[0].shape[1] // 2
    moments = tokens // (2 * rows)

    @pl.when(step == 0)
    def _():
        for chip in range(CHIPS):
            held[pl.ds(chip * width, width), :tokens] = own[chip][...]
        for relative in range(CHIPS):
            chip = jnp.bitwise_xor(where[0], relative)
            place = pl.ds(pl.multiple_of(chip * width, width), width)
            array, begin = sources[relative]
            for side in range(2):
                window = windows[relative][:, side * rows : (side + 1) * rows]
                carried = jnp.zeros(window.shape, F32)
                for moment in reversed(range(moments)):
                    at = (side * moments + moment) * rows
                    now = arrived[array][pl.ds(begin, width), pl.ds(at, rows)].astype(F32)
                    bit = jnp.bitwise_and(jnp.right_shift(window, moment), 1).astype(F32)
                    carried = bit * now + LEAK_RATE * carried
                    held[place, pl.ds(tokens + at, rows)] = carried.astype(BF16)

    value = None
    for index, act in enumerate(acts):
        term = lax.dot_general(
            act[...],
            held[:, pl.ds(index * tokens // 2, tokens // 2)],
            (((0,), (1,)), ((), ())),
            preferred_element_type=F32,
        )
        value = term if value is None else value + term
    value = value.astype(BF16)
    first, last = value[:, : 2 * width], value[:, 2 * width :]

    @pl.when(jnp.logical_or(step == 0, step == 2))
    def _():
        x_send[0] = first

    @pl.when(jnp.logical_or(step == 1, step == 3))
    def _():
        x_keep[0] = first

    @pl.when(step < 2)
    def _():
        y_send[0] = last

    @pl.when(step >= 2)
    def _():
        y_keep[0] = last


def partials(where, begin, width, membrane_t, window_t, arrived, sources, acts, rows):
    tokens = membrane_t.shape[1]
    block = 2 * rows
    specs, operands = [], []
    for chip in range(CHIPS):

        def index(i, s, chip=chip):
            return (column_block(s, jnp.bitwise_xor(s[0], chip), begin, width, rows), 0)

        specs.append(pl.BlockSpec((width, tokens), index))
        operands.append(membrane_t)
    for relative in range(CHIPS):

        def index(i, s, relative=relative):
            return (compact_block(s, relative, begin, width), 0)

        specs.append(pl.BlockSpec((width, window_t.shape[1]), index))
        operands.append(window_t)
    for array in arrived:
        specs.append(pl.BlockSpec(array.shape, lambda i, s: (0, 0)))
        operands.append(array)
    for act in acts:
        specs.append(
            pl.BlockSpec((act.shape[0], block), lambda i, s: (0, jnp.bitwise_xor(s[0], 3 - i)))
        )
        operands.append(act)
    piece = jax.ShapeDtypeStruct((2, block, 2 * width), BF16)

    def out_spec(index):
        return pl.BlockSpec((1, block, 2 * width), lambda i, s: (index(i), 0, 0))

    return pl.pallas_call(
        functools.partial(partial_kernel, sources, len(arrived), width),
        out_shape=(piece,) * 4,
        grid_spec=pltpu.PrefetchScalarGridSpec(
            num_scalar_prefetch=1,
            grid=(CHIPS,),
            in_specs=specs,
            out_specs=[
                out_spec(lambda i: jnp.where(i < 3, 1, 0)),
                out_spec(lambda i: jnp.where(i < 2, 1, 0)),
                out_spec(lambda i: jnp.where(i < 3, 1, 0)),
                out_spec(lambda i: jnp.where(i < 1, 1, 0)),
            ],
            scratch_shapes=[pltpu.VMEM((CHIPS * width, 2 * tokens), BF16)],
        ),
        cost_estimate=SMALL,
        compiler_params=pltpu.CompilerParams(vmem_limit_bytes=28 << 20),
        name="partials",
    )(where, *operands)


def gather_up_kernel(width, where, xk, xr, xs, yk, yr, ys, mine, other):
    rows = mine.shape[0]
    parts = []
    for kept, received, summed in ((xk, xr, xs), (yk, yr, ys)):
        value = kept[0].astype(F32) + received[0].astype(F32) + summed[...].astype(F32)
        parts.append(value.astype(BF16))
    value = jnp.concatenate(parts, axis=1)
    if width < LANES:
        pieces = [value[:, chip * width : (chip + 1) * width] for chip in range(CHIPS)]
        blank = jnp.zeros((value.shape[0], LANES - width), BF16)
        low = jnp.concatenate([p for piece in pieces for p in (piece, blank)], axis=1)
        high = jnp.concatenate([p for piece in pieces for p in (blank, piece)], axis=1)
        value = jnp.where(where[1] == 0, low.astype(F32), high.astype(F32)).astype(BF16)

    @pl.when(where[1] == 0)
    def _():
        mine[...] = value[:rows]
        other[...] = value[rows:]

    @pl.when(where[1] != 0)
    def _():
        mine[...] = value[rows:]
        other[...] = value[:rows]


def gather_up(where, width, kept_x, got_x, sum_x, kept_y, got_y, sum_y, rows):
    first = pl.BlockSpec((1, 2 * rows, 2 * width), lambda i, s: (0, 0, 0))
    whole = pl.BlockSpec((2 * rows, 2 * width), lambda i, s: (0, 0))
    out = jax.ShapeDtypeStruct((rows, CHIPS * LANES), BF16)
    spec = pl.BlockSpec(out.shape, lambda i, s: (0, 0))
    return pl.pallas_call(
        functools.partial(gather_up_kernel, width),
        out_shape=(out, out),
        grid_spec=pltpu.PrefetchScalarGridSpec(
            num_scalar_prefetch=1,
            grid=(1,),
            in_specs=[first, first, whole, first, first, whole],
            out_specs=[spec, spec],
        ),
        cost_estimate=SMALL,
        compiler_params=pltpu.CompilerParams(vmem_limit_bytes=12 << 20),
        name="gather_up",
    )(where, kept_x, got_x, sum_x, kept_y, got_y, sum_y)


def update_kernel(whole, where, mine, theirs, params, first, second, acts, *refs):
    fresh_params, fresh_first, fresh_second, currents = refs[-4:]
    if whole:
        own = pl.program_id(1) == where[1]
        gradient = jnp.where(own, mine[...].astype(F32), theirs[...].astype(F32))
    else:
        gradient = mine[...].astype(F32) + theirs[...].astype(F32)
    new = adam(params[...], first[...], second[...], gradient)
    fresh_params[...], fresh_first[...], fresh_second[...] = new
    currents[...] = jnp.dot(
        acts[...], new[0].astype(BF16), preferred_element_type=F32
    ).astype(BF16)


def update(where, begin, width, mine, theirs, state, acts, held):
    params = state[0]
    rows, features = params.shape
    per_chip = 2 * rows // LANES
    whole = width == LANES
    cores = 2 if whole else 1
    tile_of_core = [begin // LANES, (2 * rows - begin - width) // LANES]

    def tile(i, j, s):
        inside = jnp.where(j == 0, tile_of_core[0], tile_of_core[1])
        return (0, per_chip * i + inside)

    block = pl.BlockSpec((rows, LANES), tile)
    grads = pl.BlockSpec((rows, LANES), lambda i, j, s: (0, i))
    current_shape = jax.ShapeDtypeStruct((acts.shape[0], CHIPS * cores * LANES), BF16)
    operands = [where, mine, theirs, *state, acts]
    specs = [grads, grads, block, block, block, pl.BlockSpec(acts.shape, lambda i, j, s: (0, 0))]
    aliases = {}
    if held is not None:
        for index, array in enumerate(held):
            aliases[len(operands)] = index
            operands.append(array)
            specs.append(pl.BlockSpec(memory_space=pl.ANY))
    shape = jax.ShapeDtypeStruct((rows, features), F32)
    *fresh, currents = pl.pallas_call(
        functools.partial(update_kernel, whole),
        out_shape=(shape, shape, shape, current_shape),
        grid_spec=pltpu.PrefetchScalarGridSpec(
            num_scalar_prefetch=1,
            grid=(CHIPS, cores),
            in_specs=specs,
            out_specs=[
                block,
                block,
                block,
                pl.BlockSpec((acts.shape[0], LANES), lambda i, j, s: (0, cores * i + j)),
            ],
        ),
        input_output_aliases=aliases,
        cost_estimate=pl.CostEstimate(
            flops=2 * acts.size * CHIPS * cores * LANES,
            bytes_accessed=24 * rows * CHIPS * cores * LANES,
            transcendentals=0,
        ),
        compiler_params=pltpu.CompilerParams(vmem_limit_bytes=8 << 20),
        name="update",
    )(*operands)
    return fresh, currents


def columns_to_owners(tokens, device):
    count, features = tokens.shape
    width = features // PARTS
    cut = tokens.reshape(count, PARTS, width).transpose(1, 0, 2)
    cut = cut.reshape(2, 2, 2, count, width)
    for axis, bit in ((0, 4), (1, 2), (2, 1)):
        cut = jnp.where(jnp.bitwise_and(device, bit) != 0, jnp.flip(cut, axis), cut)
    held = cut.transpose(2, 0, 1, 3, 4)
    held = jnp.stack([held[0], over_core(held[1])])
    held = held.transpose(2, 0, 1, 3, 4)
    held = jnp.stack([held[0], over_x(held[1])])
    held = held.transpose(3 - 1, 0, 1, 3, 4)
    held = jnp.stack([held[0], over_y(held[1])])
    return held.reshape(PARTS * count, width)


def summed_to_owners(terms):
    rows, columns = terms.shape
    held = terms.reshape(CHIPS, 2, rows // PARTS, columns)

    def add(kept, got):
        return (kept.astype(F32) + got.astype(F32)).astype(BF16)

    held = add(held[:, 0], over_core(held[:, 1]))
    held = held.reshape(2, 2, rows // PARTS, columns)
    held = add(held[:, 0], over_x(held[:, 1]))
    return add(held[0], over_y(held[1]))


def relay_shards(
    master,
    first_moment,
    second_moment,
    inputs_own,
    inputs_arriving,
    grads_own,
    windows_own,
    windows_arriving,
    next_inputs,
):
    params = master[0]
    rows, features = params.shape
    steps, tok_rows = grads_own.shape[1], grads_own.shape[2]
    tokens = steps * tok_rows
    device = lax.axis_index("dp")
    core = jnp.bitwise_and(device, 1)
    where = jnp.stack([device // 2, core]).astype(jnp.int32)

    widths = [LANES] * (rows // LANES) + ([rows % LANES] if rows % LANES else [])
    begins = [sum(widths[:i]) for i in range(len(widths))]
    groups = list(zip(begins, widths))

    held = []
    for begin, width in groups:
        at = jnp.where(core == 0, begin, rows - begin - width)
        source = params if not held else tied(params, held[0])
        held.append(lax.dynamic_slice_in_dim(source, at, width, 0).astype(BF16))

    def forward(by_x, by_y, *after):
        half = by_x.shape[0] // 2
        if after:
            by_x, by_y = tied((by_x, by_y), *after)
        return over_y(by_x[:half]), over_x(by_y[half:])

    x0, y0 = over_x(held[0]), over_y(held[0])
    both = []
    for array in (grads_own, windows_own, windows_arriving):
        both.append((array[0], over_core(array[0])))
    piece = tied(held[1], both[0][1], both[1][1], both[2][1])
    x1, y1 = over_x(piece), over_y(piece)
    membrane_t, grads_t, window_t = prepare(where, *both, groups, rows)
    d0 = forward(x0, y0, membrane_t)

    (b0, w0), (b1, w1), (b2, w2) = groups

    def send(pieces, weights):
        sent = through(where, pieces, weights, membrane_t, grads_t)
        return sent, passed_along(sent, "section", -1)

    sent_a, got_a = send(
        [(0, b0, w0), (0, b1, w1), (1, b0, w0), (2, b0, w0)], [held[0], held[1], x0, y0]
    )
    piece = tied(held[2], x1, y1, sent_a)
    x2, y2 = over_x(piece), over_y(piece)
    sent_b, got_b = send(
        [(3, b0, w0), (1, b1, w1), (2, b1, w1)], [*d0, tied(x1, sent_a), y1]
    )
    acts = []
    for array in (inputs_own, inputs_arriving):
        flat = array[0].reshape(tokens, features)
        acts += [flat, over_core(tied(flat, got_a))]
    d1 = forward(x1, y1, sent_a)
    d2 = forward(x2, y2, sent_b, *d1)
    sent_c, got_c = send(
        [(3, b1, w1), (0, b2, w2), (1, b2, w2), (2, b2, w2), (3, b2, w2)],
        [*d1, held[2], tied(x2, got_a), y2, *d2],
    )

    def sum_up(g, arrived, sources, *after):
        begin, width = groups[g]
        if after:
            arrived = tied(arrived, *after)
        return partials(
            where, begin, width, membrane_t, window_t, arrived, sources, acts, rows
        )

    def first_stage(pieces, *after):
        to_x, to_y = tied((pieces[1], pieces[3]), *after) if after else (pieces[1], pieces[3])
        return over_x(to_x), over_y(to_y)

    def second_stage(pieces, got, *after):
        pass_y = (pieces[0][1].astype(F32) + got[0][1].astype(F32)).astype(BF16)
        pass_x = (pieces[2][1].astype(F32) + got[1][1].astype(F32)).astype(BF16)
        if after:
            pass_y, pass_x = tied((pass_y, pass_x), *after)
        return over_y(pass_y), over_x(pass_x), (pass_y, pass_x)

    state = (params, first_moment[0], second_moment[0])

    def finish(g, pieces, got, sums, fresh, *after):
        begin, width = groups[g]
        sum_x = tied(sums[0], *after) if after else sums[0]
        mine, other = gather_up(
            where, width, pieces[0], got[0], sum_x, pieces[2], got[1], sums[1], rows
        )
        return update(where, begin, width, mine, over_core(other), state, acts_here, fresh)

    pieces0 = sum_up(
        0, (got_a, got_b), [(0, 0), (0, w0 + w1), (0, 2 * w0 + w1), (1, 0)], sent_c
    )
    got0 = first_stage(pieces0)
    acts_here = columns_to_owners(tied(next_inputs[0], sent_c), device)
    pieces1 = sum_up(
        1, (got_a, got_b, got_c), [(0, w0), (1, w0), (1, w0 + w1), (2, 0)], pieces0[0]
    )
    sums0 = second_stage(pieces0, got0)
    got1 = first_stage(pieces1, *sums0[2])
    pieces2 = sum_up(
        2, (got_c,), [(0, w1 + r * w2) for r in range(CHIPS)], pieces1[0], *sums0[2]
    )
    got2 = first_stage(pieces2)
    fresh, current0 = finish(0, pieces0, got0, sums0, None, pieces2[0])
    sums1 = second_stage(pieces1, got1, pieces2[0], current0)
    sums2 = second_stage(pieces2, got2)
    fresh, current1 = finish(1, pieces1, got1, sums1, fresh)
    fresh, current2 = finish(2, pieces2, got2, sums2, fresh, current1)
    last = len(groups) - 1
    currents = [current0, current1, current2]

    early = summed_to_owners(jnp.concatenate(currents[:last], axis=1))
    late = summed_to_owners(currents[last])
    count = early.shape[0]
    tiles = [None] * (2 * rows // LANES)
    for g, (begin, width) in enumerate(groups):
        if g < last:
            size = CHIPS * 2 * LANES
            whole = early[:, g * size : (g + 1) * size].reshape(count, CHIPS, 2, LANES)
            tiles[begin // LANES] = whole[:, :, 0]
            tiles[(2 * rows - begin - width) // LANES] = whole[:, :, 1]
        else:
            tiles[begin // LANES] = late.reshape(count, CHIPS, LANES)
    next_currents = jnp.stack(tiles, axis=2).reshape(count, features)
    return (fresh[0][None], fresh[1][None], fresh[2][None], next_currents[None])


def membrane_grads(gradients, windows):
    carried = jnp.zeros(gradients.shape[1:], F32)
    results = []
    for moment in reversed(range(gradients.shape[0])):
        window = jnp.bitwise_and(jnp.right_shift(windows, moment), 1).astype(F32)
        carried = window * gradients[moment].astype(F32) + LEAK_RATE * carried
        results = [carried] + results
    return jnp.stack(results).astype(BF16)


def plain_shards(
    master,
    first_moment,
    second_moment,
    inputs_own,
    inputs_arriving,
    grads_own,
    windows_own,
    windows_arriving,
    next_inputs,
):
    params = master[0]
    timesteps, tok_rows, features = (grads_own.shape[1], grads_own.shape[2], grads_own.shape[3])
    flat_rows = timesteps * tok_rows
    membrane_own = membrane_grads(grads_own[0], windows_own[0]).reshape(flat_rows, features)
    weights = lax.all_gather(params.astype(BF16), "dp", axis=0, tiled=True)
    across = (((1,), (1,)), ((), ()))
    product = lax.dot_general(membrane_own, weights, across, preferred_element_type=F32)
    summed = grads_own[0].reshape(flat_rows, features).astype(F32) + product
    outgoing = summed.astype(BF16).reshape(timesteps, tok_rows, features)
    received = passed_along(outgoing, "section", -1)
    membrane_arriving = membrane_grads(received, windows_arriving[0]).reshape(flat_rows, features)
    contract = (((0,), (0,)), ((), ()))
    partial_value = lax.dot_general(
        inputs_own[0].reshape(flat_rows, features),
        membrane_own,
        contract,
        preferred_element_type=F32,
    ) + lax.dot_general(
        inputs_arriving[0].reshape(flat_rows, features),
        membrane_arriving,
        contract,
        preferred_element_type=F32,
    )
    gradient = lax.psum_scatter(
        partial_value.astype(BF16), "dp", scatter_dimension=0, tiled=True
    ).astype(F32)
    fresh_params, fresh_first, fresh_second = adam(
        params, first_moment[0], second_moment[0], gradient
    )
    gathered = lax.all_gather(fresh_params.astype(BF16), "dp", axis=0, tiled=True)
    currents = jnp.dot(next_inputs[0], gathered, preferred_element_type=F32)
    return (
        fresh_params[None],
        fresh_first[None],
        fresh_second[None],
        currents.astype(BF16)[None],
    )


def solution(mesh):
    rows = P("section", "dp", None)
    acts = P("section", None, "dp", None)
    return jax.shard_map(
        relay_shards if mesh.shape["dp"] == PARTS else plain_shards,
        mesh=mesh,
        in_specs=(rows, rows, rows, acts, acts, acts, rows, rows, rows),
        out_specs=(rows, rows, rows, rows),
        check_vma=False,
    )
```

```python
import functools

import jax
import jax.numpy as jnp
from jax import lax
from jax.experimental import pallas as pl
from jax.experimental.pallas import tpu as pltpu
from jax.sharding import PartitionSpec as P

LEAK_RATE = 0.5
LEARN_RATE = 0.002
FIRST_DECAY = 0.9
SECOND_DECAY = 0.95
EPSILON = 1e-08
WEIGHT_DECAY = 0.1
FIRST_CORRECTION = 1.0 - 0.9**10
SECOND_CORRECTION = 1.0 - 0.95**10

LANES = 128
PARTS = 8
CHIPS = 4
BF16 = jnp.bfloat16
F32 = jnp.float32


def passed_along(shard, axis, by):
    count = lax.axis_size(axis)
    pairs = [(i, i + by) for i in range(count) if 0 <= i + by < count]
    return lax.ppermute(shard, axis, pairs)


def swapped(shard, bit):
    return lax.ppermute(shard, "dp", [(i, i ^ bit) for i in range(PARTS)])


def over_core(shard):
    return swapped(shard, 1)


def over_x(shard):
    return swapped(shard, 2)


def over_y(shard):
    return swapped(shard, 4)


def over_both(shard):
    return swapped(shard, 6)


def tied(held, *earlier):
    return lax.optimization_barrier((held, *earlier))[0]


SMALL = pl.CostEstimate(flops=10**10, bytes_accessed=10**7, transcendentals=0)
VMEM = 60 << 20


def adam(params, first, second, gradient):
    fresh_first = FIRST_DECAY * first + (1.0 - FIRST_DECAY) * gradient
    fresh_second = SECOND_DECAY * second + (1.0 - SECOND_DECAY) * gradient * gradient
    direction = (
        fresh_first / FIRST_CORRECTION / (jnp.sqrt(fresh_second / SECOND_CORRECTION) + EPSILON)
    )
    fresh_params = params - LEARN_RATE * (direction + WEIGHT_DECAY * params)
    return fresh_params, fresh_first, fresh_second


def prepare_kernel(groups, where, *refs):
    grads, own, arriving = refs[0:2], refs[2:4], refs[4:6]
    membrane_t, grads_t, window_t = refs[6:]
    steps, tok_rows = grads[0].shape[0], grads[0].shape[1]
    rows = own[0].shape[1] // 2
    chip = pl.program_id(0)
    for side in range(2):
        window = own[side][...].T
        later = arriving[side][...].T
        carried = jnp.zeros(window.shape, F32)
        values = []
        for moment in reversed(range(steps)):
            now = grads[side][moment].astype(F32).T
            bit = jnp.bitwise_and(jnp.right_shift(window, moment), 1).astype(F32)
            carried = bit * now + LEAK_RATE * carried
            lanes = pl.ds((side * steps + moment) * tok_rows, tok_rows)
            membrane_t[:, lanes] = carried.astype(BF16)
            values.append((lanes, now.astype(BF16)))
        for core in range(2):

            @pl.when(where[1] == core)
            def _(core=core, later=later, values=values, side=side):
                for begin, width in groups:
                    at = begin if core == 0 else 2 * rows - begin - width
                    place = pl.ds(pl.multiple_of(CHIPS * begin + chip * width, width), width)
                    window_t[place, pl.ds(side * tok_rows, tok_rows)] = later[at : at + width]
                    for lanes, value in values:
                        grads_t[place, lanes] = value[at : at + width]


def prepare(where, grads, own, arriving, groups, rows):
    steps, tok_rows, features = grads[0].shape
    block = 2 * rows
    tokens = 2 * steps * tok_rows
    cut = CHIPS * rows
    outs = (
        jax.ShapeDtypeStruct((features, tokens), BF16),
        jax.ShapeDtypeStruct((cut, tokens), BF16),
        jax.ShapeDtypeStruct((cut, 2 * tok_rows), jnp.int32),
    )
    whole = [pl.BlockSpec(o.shape, lambda i, s: (0, 0)) for o in outs[1:]]
    return pl.pallas_call(
        functools.partial(prepare_kernel, groups),
        out_shape=outs,
        grid_spec=pltpu.PrefetchScalarGridSpec(
            num_scalar_prefetch=1,
            grid=(features // block,),
            in_specs=[pl.BlockSpec((steps, tok_rows, block), lambda i, s: (0, 0, i))] * 2
            + [pl.BlockSpec((tok_rows, block), lambda i, s: (0, i))] * 4,
            out_specs=[pl.BlockSpec((block, tokens), lambda i, s: (i, 0)), *whole],
        ),
        cost_estimate=SMALL,
        compiler_params=pltpu.CompilerParams(vmem_limit_bytes=VMEM),
        name="prepare",
    )(where, *grads, *own, *arriving)


def compact_block(s, relative, begin, width):
    return CHIPS * begin // width + jnp.bitwise_xor(s[0], relative)


def column_block(s, relative, begin, width, rows):
    chip = jnp.bitwise_xor(s[0], relative)
    at = jnp.where(s[1] == 0, begin, 2 * rows - begin - width)
    return (chip * (2 * rows) + at) // width


def through_kernel(count, pieces, where, *refs):
    weights, held = refs[:count], refs[count]
    grads = refs[count + 1 : count + 1 + len(pieces)]
    out, total = refs[count + 1 + len(pieces) :]
    step = pl.program_id(0)
    rows = jnp.concatenate([w[...] for w in weights], axis=0)
    half = held.shape[1] // 2
    for side in range(2):
        lanes = pl.ds(side * half, half)
        term = jnp.dot(rows, held[:, lanes], preferred_element_type=F32)

        @pl.when(step == 0)
        def _(lanes=lanes, term=term):
            total[:, lanes] = term

        @pl.when(step != 0)
        def _(lanes=lanes, term=term):
            at = 0
            for (_, _, width), grad in zip(pieces, grads):
                value = total[pl.ds(at, width), lanes] + term[at : at + width]
                out[pl.ds(at, width), lanes] = (value + grad[:, lanes].astype(F32)).astype(BF16)
                at += width


def through(where, pieces, weights, membrane_t, grads_t):
    features, tokens = membrane_t.shape
    count = sum(p[2] for p in pieces)
    chunk = features // 2
    out = jax.ShapeDtypeStruct((count, tokens), BF16)
    specs = [pl.BlockSpec((w.shape[0], chunk), lambda i, s: (0, i)) for w in weights]
    specs.append(pl.BlockSpec((chunk, tokens), lambda i, s: (i, 0)))
    for relative, begin, width in pieces:
        specs.append(
            pl.BlockSpec(
                (width, tokens),
                functools.partial(
                    lambda i, s, r, b, w: (compact_block(s, r, b, w), 0), r=relative, b=begin, w=width
                ),
            )
        )
    return pl.pallas_call(
        functools.partial(through_kernel, len(weights), pieces),
        out_shape=out,
        grid_spec=pltpu.PrefetchScalarGridSpec(
            num_scalar_prefetch=1,
            grid=(2,),
            in_specs=specs,
            out_specs=pl.BlockSpec((count, tokens), lambda i, s: (0, 0)),
            scratch_shapes=[pltpu.VMEM((count, tokens), F32)],
        ),
        cost_estimate=SMALL,
        compiler_params=pltpu.CompilerParams(vmem_limit_bytes=VMEM),
        name="through",
    )(where, *weights, membrane_t, *([grads_t] * len(pieces)))


def partial_kernel(sources, count, width, where, *refs):
    own, windows = refs[:CHIPS], refs[CHIPS : 2 * CHIPS]
    arrived = refs[2 * CHIPS : 2 * CHIPS + count]
    refs = refs[2 * CHIPS + count :]
    acts = refs[:4]
    x_keep, x_send, y_keep, y_send, held = refs[4:]
    step = pl.program_id(0)
    tokens = own[0].shape[1]
    rows = windows[0].shape[1] // 2
    moments = tokens // (2 * rows)

    @pl.when(step == 0)
    def _():
        for chip in range(CHIPS):
            held[pl.ds(chip * width, width), :tokens] = own[chip][...]
        for relative in range(CHIPS):
            chip = jnp.bitwise_xor(where[0], relative)
            place = pl.ds(pl.multiple_of(chip * width, width), width)
            array, begin = sources[relative]
            for side in range(2):
                window = windows[relative][:, side * rows : (side + 1) * rows]
                carried = jnp.zeros(window.shape, F32)
                for moment in reversed(range(moments)):
                    at = (side * moments + moment) * rows
                    now = arrived[array][pl.ds(begin, width), pl.ds(at, rows)].astype(F32)
                    bit = jnp.bitwise_and(jnp.right_shift(window, moment), 1).astype(F32)
                    carried = bit * now + LEAK_RATE * carried
                    held[place, pl.ds(tokens + at, rows)] = carried.astype(BF16)

    value = None
    for index, act in enumerate(acts):
        term = lax.dot_general(
            act[...],
            held[:, pl.ds(index * tokens // 2, tokens // 2)],
            (((0,), (1,)), ((), ())),
            preferred_element_type=F32,
        )
        value = term if value is None else value + term
    value = value.astype(BF16)
    first, last = value[:, : 2 * width], value[:, 2 * width :]

    @pl.when(jnp.logical_or(step == 0, step == 2))
    def _():
        x_send[0] = first

    @pl.when(jnp.logical_or(step == 1, step == 3))
    def _():
        x_keep[0] = first

    @pl.when(step < 2)
    def _():
        y_send[0] = last

    @pl.when(step >= 2)
    def _():
        y_keep[0] = last


def partials(where, begin, width, membrane_t, window_t, arrived, sources, acts, rows):
    tokens = membrane_t.shape[1]
    block = 2 * rows
    specs, operands = [], []
    for chip in range(CHIPS):

        def index(i, s, chip=chip):
            return (column_block(s, jnp.bitwise_xor(s[0], chip), begin, width, rows), 0)

        specs.append(pl.BlockSpec((width, tokens), index))
        operands.append(membrane_t)
    for relative in range(CHIPS):

        def index(i, s, relative=relative):
            return (compact_block(s, relative, begin, width), 0)

        specs.append(pl.BlockSpec((width, window_t.shape[1]), index))
        operands.append(window_t)
    for array in arrived:
        specs.append(pl.BlockSpec(array.shape, lambda i, s: (0, 0)))
        operands.append(array)
    for act in acts:
        specs.append(
            pl.BlockSpec((act.shape[0], block), lambda i, s: (0, jnp.bitwise_xor(s[0], 3 - i)))
        )
        operands.append(act)
    piece = jax.ShapeDtypeStruct((2, block, 2 * width), BF16)

    def out_spec(index):
        return pl.BlockSpec((1, block, 2 * width), lambda i, s: (index(i), 0, 0))

    return pl.pallas_call(
        functools.partial(partial_kernel, sources, len(arrived), width),
        out_shape=(piece,) * 4,
        grid_spec=pltpu.PrefetchScalarGridSpec(
            num_scalar_prefetch=1,
            grid=(CHIPS,),
            in_specs=specs,
            out_specs=[
                out_spec(lambda i: jnp.where(i < 3, 1, 0)),
                out_spec(lambda i: jnp.where(i < 2, 1, 0)),
                out_spec(lambda i: jnp.where(i < 3, 1, 0)),
                out_spec(lambda i: jnp.where(i < 1, 1, 0)),
            ],
            scratch_shapes=[pltpu.VMEM((CHIPS * width, 2 * tokens), BF16)],
        ),
        cost_estimate=SMALL,
        compiler_params=pltpu.CompilerParams(vmem_limit_bytes=28 << 20),
        name="partials",
    )(where, *operands)


def gather_up_kernel(width, where, xk, xr, xs, yk, yr, ys, mine, other):
    rows = mine.shape[0]
    parts = []
    for kept, received, summed in ((xk, xr, xs), (yk, yr, ys)):
        value = kept[0].astype(F32) + received[0].astype(F32) + summed[...].astype(F32)
        parts.append(value.astype(BF16))
    value = jnp.concatenate(parts, axis=1)
    if width < LANES:
        pieces = [value[:, chip * width : (chip + 1) * width] for chip in range(CHIPS)]
        blank = jnp.zeros((value.shape[0], LANES - width), BF16)
        low = jnp.concatenate([p for piece in pieces for p in (piece, blank)], axis=1)
        high = jnp.concatenate([p for piece in pieces for p in (blank, piece)], axis=1)
        value = jnp.where(where[1] == 0, low.astype(F32), high.astype(F32)).astype(BF16)

    @pl.when(where[1] == 0)
    def _():
        mine[...] = value[:rows]
        other[...] = value[rows:]

    @pl.when(where[1] != 0)
    def _():
        mine[...] = value[rows:]
        other[...] = value[:rows]


def gather_up(where, width, kept_x, got_x, sum_x, kept_y, got_y, sum_y, rows):
    first = pl.BlockSpec((1, 2 * rows, 2 * width), lambda i, s: (0, 0, 0))
    whole = pl.BlockSpec((2 * rows, 2 * width), lambda i, s: (0, 0))
    out = jax.ShapeDtypeStruct((rows, CHIPS * LANES), BF16)
    spec = pl.BlockSpec(out.shape, lambda i, s: (0, 0))
    return pl.pallas_call(
        functools.partial(gather_up_kernel, width),
        out_shape=(out, out),
        grid_spec=pltpu.PrefetchScalarGridSpec(
            num_scalar_prefetch=1,
            grid=(1,),
            in_specs=[first, first, whole, first, first, whole],
            out_specs=[spec, spec],
        ),
        cost_estimate=SMALL,
        compiler_params=pltpu.CompilerParams(vmem_limit_bytes=12 << 20),
        name="gather_up",
    )(where, kept_x, got_x, sum_x, kept_y, got_y, sum_y)


def update_kernel(whole, where, mine, theirs, params, first, second, acts, *refs):
    fresh_params, fresh_first, fresh_second, currents = refs[-4:]
    if whole:
        own = pl.program_id(1) == where[1]
        gradient = jnp.where(own, mine[...].astype(F32), theirs[...].astype(F32))
    else:
        gradient = mine[...].astype(F32) + theirs[...].astype(F32)
    new = adam(params[...], first[...], second[...], gradient)
    fresh_params[...], fresh_first[...], fresh_second[...] = new
    currents[...] = jnp.dot(
        acts[...], new[0].astype(BF16), preferred_element_type=F32
    ).astype(BF16)


def update(where, begin, width, mine, theirs, state, acts, held):
    params = state[0]
    rows, features = params.shape
    per_chip = 2 * rows // LANES
    whole = width == LANES
    cores = 2 if whole else 1
    tile_of_core = [begin // LANES, (2 * rows - begin - width) // LANES]

    def tile(i, j, s):
        inside = jnp.where(j == 0, tile_of_core[0], tile_of_core[1])
        return (0, per_chip * i + inside)

    block = pl.BlockSpec((rows, LANES), tile)
    grads = pl.BlockSpec((rows, LANES), lambda i, j, s: (0, i))
    current_shape = jax.ShapeDtypeStruct((acts.shape[0], CHIPS * cores * LANES), BF16)
    operands = [where, mine, theirs, *state, acts]
    specs = [grads, grads, block, block, block, pl.BlockSpec(acts.shape, lambda i, j, s: (0, 0))]
    aliases = {}
    if held is not None:
        for index, array in enumerate(held):
            aliases[len(operands)] = index
            operands.append(array)
            specs.append(pl.BlockSpec(memory_space=pl.ANY))
    shape = jax.ShapeDtypeStruct((rows, features), F32)
    *fresh, currents = pl.pallas_call(
        functools.partial(update_kernel, whole),
        out_shape=(shape, shape, shape, current_shape),
        grid_spec=pltpu.PrefetchScalarGridSpec(
            num_scalar_prefetch=1,
            grid=(CHIPS, cores),
            in_specs=specs,
            out_specs=[
                block,
                block,
                block,
                pl.BlockSpec((acts.shape[0], LANES), lambda i, j, s: (0, cores * i + j)),
            ],
        ),
        input_output_aliases=aliases,
        cost_estimate=pl.CostEstimate(
            flops=2 * acts.size * CHIPS * cores * LANES,
            bytes_accessed=24 * rows * CHIPS * cores * LANES,
            transcendentals=0,
        ),
        compiler_params=pltpu.CompilerParams(vmem_limit_bytes=8 << 20),
        name="update",
    )(*operands)
    return fresh, currents


def columns_to_owners(tokens, device):
    count, features = tokens.shape
    width = features // PARTS
    cut = tokens.reshape(count, PARTS, width).transpose(1, 0, 2)
    cut = cut.reshape(2, 2, 2, count, width)
    for axis, bit in ((0, 4), (1, 2), (2, 1)):
        cut = jnp.where(jnp.bitwise_and(device, bit) != 0, jnp.flip(cut, axis), cut)
    held = cut.transpose(2, 0, 1, 3, 4)
    held = jnp.stack([held[0], over_core(held[1])])
    held = held.transpose(2, 0, 1, 3, 4)
    held = jnp.stack([held[0], over_x(held[1])])
    held = held.transpose(3 - 1, 0, 1, 3, 4)
    held = jnp.stack([held[0], over_y(held[1])])
    return held.reshape(PARTS * count, width)


def summed_to_owners(terms):
    rows, columns = terms.shape
    held = terms.reshape(CHIPS, 2, rows // PARTS, columns)

    def add(kept, got):
        return (kept.astype(F32) + got.astype(F32)).astype(BF16)

    held = add(held[:, 0], over_core(held[:, 1]))
    near = held[0].astype(F32) + over_x(held[1]).astype(F32)
    far = over_y(held[2]).astype(F32) + over_both(held[3]).astype(F32)
    return (near + far).astype(BF16)


def relay_shards(
    master,
    first_moment,
    second_moment,
    inputs_own,
    inputs_arriving,
    grads_own,
    windows_own,
    windows_arriving,
    next_inputs,
):
    params = master[0]
    rows, features = params.shape
    steps, tok_rows = grads_own.shape[1], grads_own.shape[2]
    tokens = steps * tok_rows
    device = lax.axis_index("dp")
    core = jnp.bitwise_and(device, 1)
    where = jnp.stack([device // 2, core]).astype(jnp.int32)

    widths = [LANES] * (rows // LANES) + ([rows % LANES] if rows % LANES else [])
    begins = [sum(widths[:i]) for i in range(len(widths))]
    groups = list(zip(begins, widths))

    held = []
    for begin, width in groups:
        at = jnp.where(core == 0, begin, rows - begin - width)
        source = params if not held else tied(params, held[0])
        held.append(lax.dynamic_slice_in_dim(source, at, width, 0).astype(BF16))

    def forward(by_x, by_y, *after):
        half = by_x.shape[0] // 2
        if after:
            by_x, by_y = tied((by_x, by_y), *after)
        return over_y(by_x[:half]), over_x(by_y[half:])

    x0, y0 = over_x(held[0]), over_y(held[0])
    both = []
    for array in (grads_own, windows_own, windows_arriving):
        both.append((array[0], over_core(array[0])))
    piece = tied(held[1], both[0][1], both[1][1], both[2][1])
    x1, y1 = over_x(piece), over_y(piece)
    membrane_t, grads_t, window_t = prepare(where, *both, groups, rows)
    d0 = forward(x0, y0, membrane_t)

    (b0, w0), (b1, w1), (b2, w2) = groups

    def send(pieces, weights):
        sent = through(where, pieces, weights, membrane_t, grads_t)
        return sent, passed_along(sent, "section", -1)

    sent_a, got_a = send(
        [(0, b0, w0), (0, b1, w1), (1, b0, w0), (2, b0, w0)], [held[0], held[1], x0, y0]
    )
    piece = tied(held[2], x1, y1, sent_a)
    x2, y2 = over_x(piece), over_y(piece)
    sent_b, got_b = send(
        [(3, b0, w0), (1, b1, w1), (2, b1, w1)], [*d0, tied(x1, sent_a), y1]
    )
    acts = []
    for array in (inputs_own, inputs_arriving):
        flat = array[0].reshape(tokens, features)
        acts += [flat, over_core(tied(flat, got_a))]
    d1 = forward(x1, y1, sent_a)
    d2 = forward(x2, y2, sent_b, *d1)
    sent_c, got_c = send(
        [(3, b1, w1), (0, b2, w2), (1, b2, w2), (2, b2, w2), (3, b2, w2)],
        [*d1, held[2], tied(x2, got_a), y2, *d2],
    )

    def sum_up(g, arrived, sources, *after):
        begin, width = groups[g]
        if after:
            arrived = tied(arrived, *after)
        return partials(
            where, begin, width, membrane_t, window_t, arrived, sources, acts, rows
        )

    def first_stage(pieces, *after):
        to_x, to_y = tied((pieces[1], pieces[3]), *after) if after else (pieces[1], pieces[3])
        return over_x(to_x), over_y(to_y)

    def second_stage(pieces, got, *after):
        pass_y = (pieces[0][1].astype(F32) + got[0][1].astype(F32)).astype(BF16)
        pass_x = (pieces[2][1].astype(F32) + got[1][1].astype(F32)).astype(BF16)
        if after:
            pass_y, pass_x = tied((pass_y, pass_x), *after)
        return over_y(pass_y), over_x(pass_x), (pass_y, pass_x)

    state = (params, first_moment[0], second_moment[0])

    def finish(g, pieces, got, sums, fresh, *after):
        begin, width = groups[g]
        sum_x = tied(sums[0], *after) if after else sums[0]
        mine, other = gather_up(
            where, width, pieces[0], got[0], sum_x, pieces[2], got[1], sums[1], rows
        )
        return update(where, begin, width, mine, over_core(other), state, acts_here, fresh)

    pieces0 = sum_up(
        0, (got_a, got_b), [(0, 0), (0, w0 + w1), (0, 2 * w0 + w1), (1, 0)], sent_c
    )
    got0 = first_stage(pieces0)
    acts_here = columns_to_owners(tied(next_inputs[0], sent_c), device)
    pieces1 = sum_up(
        1, (got_a, got_b, got_c), [(0, w0), (1, w0), (1, w0 + w1), (2, 0)], pieces0[0]
    )
    sums0 = second_stage(pieces0, got0)
    got1 = first_stage(pieces1, *sums0[2])
    pieces2 = sum_up(
        2, (got_c,), [(0, w1 + r * w2) for r in range(CHIPS)], pieces1[0], *sums0[2]
    )
    got2 = first_stage(pieces2)
    fresh, current0 = finish(0, pieces0, got0, sums0, None, pieces2[0])
    sums1 = second_stage(pieces1, got1, pieces2[0], current0)
    sums2 = second_stage(pieces2, got2)
    fresh, current1 = finish(1, pieces1, got1, sums1, fresh)
    fresh, current2 = finish(2, pieces2, got2, sums2, fresh, current1)
    last = len(groups) - 1
    currents = [current0, current1, current2]

    early = summed_to_owners(jnp.concatenate(currents[:last], axis=1))
    late = summed_to_owners(currents[last])
    count = early.shape[0]
    tiles = [None] * (2 * rows // LANES)
    for g, (begin, width) in enumerate(groups):
        if g < last:
            size = CHIPS * 2 * LANES
            whole = early[:, g * size : (g + 1) * size].reshape(count, CHIPS, 2, LANES)
            tiles[begin // LANES] = whole[:, :, 0]
            tiles[(2 * rows - begin - width) // LANES] = whole[:, :, 1]
        else:
            tiles[begin // LANES] = late.reshape(count, CHIPS, LANES)
    next_currents = jnp.stack(tiles, axis=2).reshape(count, features)
    return (fresh[0][None], fresh[1][None], fresh[2][None], next_currents[None])


def membrane_grads(gradients, windows):
    carried = jnp.zeros(gradients.shape[1:], F32)
    results = []
    for moment in reversed(range(gradients.shape[0])):
        window = jnp.bitwise_and(jnp.right_shift(windows, moment), 1).astype(F32)
        carried = window * gradients[moment].astype(F32) + LEAK_RATE * carried
        results = [carried] + results
    return jnp.stack(results).astype(BF16)


def plain_shards(
    master,
    first_moment,
    second_moment,
    inputs_own,
    inputs_arriving,
    grads_own,
    windows_own,
    windows_arriving,
    next_inputs,
):
    params = master[0]
    timesteps, tok_rows, features = (grads_own.shape[1], grads_own.shape[2], grads_own.shape[3])
    flat_rows = timesteps * tok_rows
    membrane_own = membrane_grads(grads_own[0], windows_own[0]).reshape(flat_rows, features)
    weights = lax.all_gather(params.astype(BF16), "dp", axis=0, tiled=True)
    across = (((1,), (1,)), ((), ()))
    product = lax.dot_general(membrane_own, weights, across, preferred_element_type=F32)
    summed = grads_own[0].reshape(flat_rows, features).astype(F32) + product
    outgoing = summed.astype(BF16).reshape(timesteps, tok_rows, features)
    received = passed_along(outgoing, "section", -1)
    membrane_arriving = membrane_grads(received, windows_arriving[0]).reshape(flat_rows, features)
    contract = (((0,), (0,)), ((), ()))
    partial_value = lax.dot_general(
        inputs_own[0].reshape(flat_rows, features),
        membrane_own,
        contract,
        preferred_element_type=F32,
    ) + lax.dot_general(
        inputs_arriving[0].reshape(flat_rows, features),
        membrane_arriving,
        contract,
        preferred_element_type=F32,
    )
    gradient = lax.psum_scatter(
        partial_value.astype(BF16), "dp", scatter_dimension=0, tiled=True
    ).astype(F32)
    fresh_params, fresh_first, fresh_second = adam(
        params, first_moment[0], second_moment[0], gradient
    )
    gathered = lax.all_gather(fresh_params.astype(BF16), "dp", axis=0, tiled=True)
    currents = jnp.dot(next_inputs[0], gathered, preferred_element_type=F32)
    return (
        fresh_params[None],
        fresh_first[None],
        fresh_second[None],
        currents.astype(BF16)[None],
    )


def solution(mesh):
    rows = P("section", "dp", None)
    acts = P("section", None, "dp", None)
    return jax.shard_map(
        relay_shards if mesh.shape["dp"] == PARTS else plain_shards,
        mesh=mesh,
        in_specs=(rows, rows, rows, acts, acts, acts, rows, rows, rows),
        out_specs=(rows, rows, rows, rows),
        check_vma=False,
    )
```
